32 devices in a mesh: rep: 2 (over y), gx: 4 (over z), gy: 4 (over x, core).
Axes of the slice: x: 2, y: 2, z: 4, core: 2. Of those that a mesh axis runs over, the one named last changes fastest.
Arguments:
- residual: bfloat16 [64, 16384], P('rep', 'gx'), parts along dimension 0, may hold values from -1.5 to 1.5
- ffn_partial: float32 [4, 64, 16384], P('gy', 'rep', 'gx'), parts along dimension 1, may hold values from -1.5 to 1.5
- norm_gain: float32 [16384], P('gx'), may hold values from 0.1 to 1.9
- smooth_scale: float32 [16384], P('gx'), may hold values from 0.25 to 4
- w_query: bfloat16 [16384, 8192], P('gx', 'gy'), may hold values from -127 to 127, as said below
- query_scale: float32 [8192], P('gy'), may hold values from 3.125e-05 to 0.000125
- w_keyval: bfloat16 [16384, 1024], P('gx', 'gy'), may hold values from -127 to 127, as said below
- keyval_scale: float32 [1024], P('gy'), may hold values from 3.125e-05 to 0.000125
- key_cache: bfloat16 [64, 4, 512, 128], P(('rep', 'gy'), None, 'gx'), parts along dimension 0, may hold values from -127 to 127, as said below
- value_cache: bfloat16 [64, 4, 512, 128], P(('rep', 'gy'), None, 'gx'), parts along dimension 0, may hold values from -127 to 127, as said below
- key_scale: float32 [64, 4, 512], P(('rep', 'gy'), None, 'gx'), parts along dimension 0, may hold values from 0.007 to 8
- value_scale: float32 [64, 4, 512], P(('rep', 'gy'), None, 'gx'), parts along dimension 0, may hold values from 0.007 to 0.027
- lengths: int32 [64], P(('rep', 'gy')), parts along dimension 0, may hold values from 1 to 512, as said below
- w_out: bfloat16 [8192, 16384], P('gy', 'gx'), may hold values from -127 to 127, as said below
- out_scale: float32 [16384], P('gx'), may hold values from 0.00030935922 to 0.0011932427
Outputs:
- new_residual: bfloat16 [64, 16384], P('rep', 'gx'), parts along dimension 0
The draws below stay inside these ranges and needn't reach their ends.
There are 2 independent parts, one for each index of `rep`. The reference program is written for one: setup_inputs(seed, part) draws one part's arguments, and reference() takes and returns one part's arrays. A program takes and returns all parts, laid end to end along the dimension named above; an argument that names none is the same for every part. Nothing has to cross between parts.
Inputs may be any that keep to these rules, and one draw needn't show every extreme that they name: `w_query`: integer codes of the weights. `w_keyval`: integer codes of the weights. `w_out`: integer codes of the weights. `key_cache`: integer codes. `value_cache`: integer codes. `lengths`: some request uses all 512 positions and some request uses one.
All inputs are finite; a program needn't handle non-finite values.
Results may differ from the reference program's by a relative error of at most 0.011.
Values may be sent and summed in bfloat16 or wider, within the bound.
No kernel may reach another device: no remote copies, remote signals or barrier semaphores. Data moves between devices by JAX's collectives and lax.ppermute only.
A program may use at most 128 MiB of HBM per device.

```python
import math
import jax
import jax.numpy as jnp
from jax import lax

D = 16384
HEADS = 64
KV_HEADS = 4
HEAD_DIM = 128
ROWS = 32
CACHE = 512
N_GY = 4


def integer_codes(key, tensor_shape):
    return jax.random.randint(key, tensor_shape, -127, 128).astype(jnp.float32).astype(jnp.bfloat16)


def draw_w_query(key, part):
    key = jax.random.fold_in(key, 11)
    return integer_codes(key, (D, HEADS * HEAD_DIM))


def draw_w_keyval(key, part):
    key = jax.random.fold_in(key, 12)
    return integer_codes(key, (D, 2 * KV_HEADS * HEAD_DIM))


def draw_w_out(key, part):
    key = jax.random.fold_in(key, 13)
    return integer_codes(key, (HEADS * HEAD_DIM, D))


def draw_key_cache(key, part):
    key = jax.random.fold_in(key, 14)
    return integer_codes(key, (ROWS, KV_HEADS, CACHE, HEAD_DIM))


def draw_value_cache(key, part):
    key = jax.random.fold_in(key, 15)
    return integer_codes(key, (ROWS, KV_HEADS, CACHE, HEAD_DIM))


def draw_key_scale(key, part):
    key = jax.random.fold_in(key, 16)
    tensor_shape = (ROWS, KV_HEADS, CACHE)
    random_seed_key = jax.random.fold_in(key, 0)
    return jnp.exp(jax.random.uniform(random_seed_key, tensor_shape, jnp.float32, math.log(0.007), math.log(0.027)))


def draw_lengths(key, part):
    key = jax.random.fold_in(key, 17)
    body_key, first_key, second_key = jax.random.split(key, 3)
    drawn = jax.random.randint(body_key, (ROWS,), 1, CACHE + 1)
    longest = jax.random.randint(first_key, (), 0, ROWS)
    shortest = (longest + 1 + jax.random.randint(second_key, (), 0, ROWS - 1)) % ROWS
    places = jnp.arange(ROWS, dtype=jnp.int32)
    drawn = jnp.where(places == longest, CACHE, drawn)
    return jnp.where(places == shortest, 1, drawn).astype(jnp.int32)


def spiked(values, rng, source, target, shards_of, factor):
    def block_of(axis_at):
        return (jnp.arange(values.shape[axis_at]) // (values.shape[axis_at] // shards_of)).reshape((-1,) + (1,) * (values.ndim - 1 - axis_at))

    near = jax.random.permutation(rng, shards_of)[block_of(target)]
    other_side = (block_of(target) + shards_of // 2) % shards_of
    return jnp.where((block_of(source) == near) | (block_of(source) == other_side), factor * values, values)


def block_levels(stream_key, shape, cuts, least, high):
    loudness = 1.0
    for axis_at, parts in cuts:
        steps = jax.random.uniform(jax.random.fold_in(jax.random.fold_in(stream_key, 6), axis_at), (parts,), jnp.float32, least / len(cuts), high / len(cuts))
        loudness = loudness * jnp.repeat(jnp.exp(steps), shape[axis_at] // parts).reshape((-1,) + (1,) * (len(shape) - 1 - axis_at))
    return loudness


def normal_values(own_key, shape, spread, reach, cuts=(), held_as=jnp.bfloat16):
    loudness = block_levels(own_key, shape, cuts, -0.22, 0.18) if cuts else 1.0
    array = jax.random.normal(own_key, shape, jnp.float32) * spread * loudness
    return jnp.minimum(jnp.maximum(array, -reach), reach).astype(held_as)


def gaussian_with(rng, extent, width, bound, shards, heavy, kind=jnp.bfloat16):
    values = width * jax.random.normal(rng, extent, jnp.float32)
    if shards:
        values = values * block_levels(rng, extent, shards, -0.22, 0.18)
    return jnp.clip(spiked(values, jax.random.fold_in(rng, 3), *heavy), -bound, bound).astype(kind)


def setup_inputs(seed: int = 0, part: int = 0) -> dict:
    key_list = jax.random.split(jax.random.key(seed), 16)
    part_splits = jax.random.split(jax.random.fold_in(key_list[15], part), 16)
    residual = normal_values(part_splits[0], (ROWS, D), 0.25, 1.5, ((1, 4),))
    ffn_partial = gaussian_with(part_splits[1], (N_GY, ROWS, D), 0.25, 1.5, ((0, 4), (2, 4)), (0, 2, 4, 2.0), jnp.float32)
    norm_gain = jnp.clip(1.0 + 0.18 * jax.random.normal(key_list[2], (D,), jnp.float32), 0.1, 1.9)
    smooth_scale = jnp.clip(jnp.exp(math.log(4.0) - 2.7725887 * jax.random.uniform(key_list[3], (D,), jnp.float32) ** block_levels(key_list[3], (D,), ((0, 4),), -0.2, 0.2)), 0.25, 4.0)
    w_query = draw_w_query(jax.random.fold_in(key_list[15], 71), part)
    query_scale = jnp.clip(jnp.exp(math.log(0.000125) - 1.3862944 * jax.random.uniform(key_list[5], (HEADS * HEAD_DIM,), jnp.float32) ** block_levels(key_list[5], (HEADS * HEAD_DIM,), ((0, 4),), -0.2, 0.2)), 3.125000148429535e-05, 0.000125)
    w_keyval = draw_w_keyval(jax.random.fold_in(key_list[15], 71), part)
    keyval_scale = jnp.clip(jnp.exp(math.log(0.000125) - 1.3862944 * jax.random.uniform(key_list[7], (2 * KV_HEADS * HEAD_DIM,), jnp.float32) ** block_levels(key_list[7], (2 * KV_HEADS * HEAD_DIM,), ((0, 4),), -0.2, 0.2)), 3.125000148429535e-05, 0.000125)
    key_cache = draw_key_cache(jax.random.fold_in(jax.random.fold_in(key_list[15], part), 71), part)
    value_cache = draw_value_cache(jax.random.fold_in(jax.random.fold_in(key_list[15], part), 71), part)
    key_scale = draw_key_scale(jax.random.fold_in(jax.random.fold_in(key_list[15], part), 71), part)
    value_scale = jnp.clip(jnp.exp(math.log(0.027) - 1.3499267 * jax.random.uniform(part_splits[11], (ROWS, KV_HEADS, CACHE), jnp.float32) ** block_levels(part_splits[11], (ROWS, KV_HEADS, CACHE), ((0, 4), (2, 4)), -0.2, 0.2)), 0.007, 0.027)
    lengths = draw_lengths(jax.random.fold_in(jax.random.fold_in(key_list[15], part), 71), part)
    w_out = draw_w_out(jax.random.fold_in(key_list[15], 71), part)
    out_scale = jnp.clip(jnp.exp(math.log(0.0011932427) - 1.3499267 * jax.random.uniform(key_list[14], (D,), jnp.float32) ** block_levels(key_list[14], (D,), ((0, 4),), -0.2, 0.2)), 0.00030935922, 0.0011932427)
    return dict(residual=residual, ffn_partial=ffn_partial, norm_gain=norm_gain, smooth_scale=smooth_scale, w_query=w_query, query_scale=query_scale, w_keyval=w_keyval, keyval_scale=keyval_scale, key_cache=key_cache, value_cache=value_cache, key_scale=key_scale, value_scale=value_scale, lengths=lengths, w_out=w_out, out_scale=out_scale)


EPSILON = 1e-05
NEGATIVE = -1e+30

def attend_row(input_rows):
    query_vectors, fresh_key_rows, fresh_value_rows, key_vectors, value_vectors, key_dequant_scale, value_dequant_scale, length_limit = input_rows
    score_multiplier = HEAD_DIM ** (-0.5)
    logit_scores = jnp.einsum('gqd,gsd->gqs', query_vectors.astype(jnp.float32), key_vectors.astype(jnp.float32))
    logit_scores = logit_scores * key_dequant_scale[:, None, :] * score_multiplier
    visible = (jnp.arange(CACHE, dtype=jnp.int32) < length_limit)[None, None, :]
    logit_scores = jnp.where(visible, logit_scores, NEGATIVE)
    own = jnp.einsum('gqd,gd->gq', query_vectors.astype(jnp.float32), fresh_key_rows.astype(jnp.float32)) * score_multiplier
    largest = jnp.maximum(lax.optimization_barrier(jnp.max(logit_scores, axis=-1)), own)
    weights = jnp.where(visible, jnp.exp(logit_scores - largest[..., None]), 0.0)
    own_weight = jnp.exp(own - largest)
    total = lax.optimization_barrier(jnp.sum(weights, axis=-1)) + own_weight
    scaled = (weights * value_dequant_scale[:, None, :]).astype(jnp.bfloat16)
    mixed = jnp.einsum('gqs,gsd->gqd', scaled.astype(jnp.float32), value_vectors.astype(jnp.float32))
    mixed = mixed + own_weight[..., None] * fresh_value_rows.astype(jnp.float32)[:, None, :]
    return (mixed / total[..., None]).astype(jnp.bfloat16)

def reference(residual, ffn_partial, norm_gain, smooth_scale, w_query, query_scale, w_keyval, keyval_scale, key_cache, value_cache, key_scale, value_scale, lengths, w_out, out_scale):
    widened = residual.astype(jnp.float32)
    squares = lax.optimization_barrier(jnp.sum(widened * widened, axis=1))
    row_scale = lax.rsqrt(squares / D + EPSILON)[:, None]
    smoothed = (widened * (norm_gain / smooth_scale)).astype(jnp.bfloat16)
    query_vectors = (row_scale * (jnp.dot(smoothed, w_query, preferred_element_type=jnp.float32) * query_scale)).astype(jnp.bfloat16)
    keyvals = (row_scale * (jnp.dot(smoothed, w_keyval, preferred_element_type=jnp.float32) * keyval_scale)).astype(jnp.bfloat16)
    group = HEADS // KV_HEADS
    grouped = query_vectors.reshape(ROWS, KV_HEADS, group, HEAD_DIM)
    fresh_key_rows = keyvals[:, :KV_HEADS * HEAD_DIM].reshape(ROWS, KV_HEADS, HEAD_DIM)
    fresh_value_rows = keyvals[:, KV_HEADS * HEAD_DIM:].reshape(ROWS, KV_HEADS, HEAD_DIM)
    attended = lax.map(attend_row, (grouped, fresh_key_rows, fresh_value_rows, key_cache, value_cache, key_scale, value_scale, lengths))
    attended = attended.reshape(ROWS, HEADS * HEAD_DIM)
    projected = jnp.dot(attended, w_out, preferred_element_type=jnp.float32) * out_scale
    return (widened + lax.optimization_barrier(jnp.sum(ffn_partial, axis=0)) + projected).astype(jnp.bfloat16)
```

```python
import jax
import jax.numpy as jnp
from jax import lax
from jax.sharding import PartitionSpec as P

D = 16384
HEADS = 64
KV_HEADS = 4
HEAD_DIM = 128
GROUP = HEADS // KV_HEADS
EPSILON = 1e-05
NEGATIVE = -1e30
f32 = jnp.float32
bf16 = jnp.bfloat16


def partners(n, offset):
    return [(i, i ^ offset) for i in range(n)]


def ordered(pieces, me):
    n = len(pieces)
    return [lax.select_n(me, *[pieces[j ^ i] for i in range(n)]) for j in range(n)]


def exchange(chunks, axis, n):
    me = lax.axis_index(axis)
    own = lax.dynamic_index_in_dim(chunks, me, 0, keepdims=False)
    return [own] + [
        lax.ppermute(lax.dynamic_index_in_dim(chunks, me ^ k, 0, keepdims=False), axis, partners(n, k))
        for k in range(1, n)
    ]


def gather(value, axis, n):
    return [value] + [lax.ppermute(value, axis, partners(n, k)) for k in range(1, n)]


def swap(value, axis, n, offset):
    return lax.ppermute(value, axis, partners(n, offset))


def body(n_gx, n_gy, residual, ffn_partial, norm_gain, smooth_scale, w_query, query_scale, w_keyval, keyval_scale,
         key_cache, value_cache, key_scale, value_scale, lengths, w_out, out_scale):
    gx, gy = lax.axis_index("gx"), lax.axis_index("gy")
    rows, width = residual.shape
    requests = rows // n_gy
    widened = residual.astype(f32)
    squares = jnp.sum(widened * widened, axis=1)
    smoothed = (widened * (norm_gain / smooth_scale)).astype(bf16)
    query_part = jnp.dot(smoothed, w_query, preferred_element_type=f32) * query_scale
    keyval_part = jnp.dot(smoothed, w_keyval, preferred_element_type=f32) * keyval_scale
    qc, kc = query_part.shape[1] // n_gx, keyval_part.shape[1] // n_gx
    pad = -(qc + kc + 1) % 128
    packed = jnp.concatenate([
        query_part.reshape(rows, n_gx, qc), keyval_part.reshape(rows, n_gx, kc),
        jnp.broadcast_to(squares[:, None, None], (rows, n_gx, 1)), jnp.zeros((rows, n_gx, pad), f32)], axis=2)
    pieces = exchange(packed.transpose(1, 0, 2), "gx", n_gx)
    summed = sum(pieces[1:], pieces[0])
    row_scale = lax.rsqrt(summed[:, qc + kc] / D + EPSILON)[:, None]
    rounded = (row_scale * summed).astype(bf16)[:, : qc + kc]
    rounded = jnp.pad(rounded, ((0, 0), (0, pad + 1)))
    mine = jnp.stack(ordered(exchange(rounded.reshape(n_gy, requests, -1), "gy", n_gy), gy))
    everything = jnp.stack(ordered(gather(mine, "gx", n_gx), gx))
    query_vectors = everything[..., :qc].transpose(2, 1, 0, 3).reshape(requests, KV_HEADS, GROUP, HEAD_DIM)
    keyvals = everything[..., qc : qc + kc].transpose(2, 1, 0, 3).reshape(requests, 2 * KV_HEADS, HEAD_DIM)
    fresh_keys, fresh_values = keyvals[:, :KV_HEADS], keyvals[:, KV_HEADS:]

    local = key_cache.shape[2]
    multiplier = HEAD_DIM ** (-0.5)
    logits = jnp.einsum("rgqd,rgsd->rgqs", query_vectors, key_cache, preferred_element_type=f32)
    logits = logits * key_scale[:, :, None, :] * multiplier
    position = gx * local + jnp.arange(local, dtype=jnp.int32)
    visible = (position[None, :] < lengths[:, None])[:, None, None, :]
    logits = jnp.where(visible, logits, NEGATIVE)
    own = jnp.einsum("rgqd,rgd->rgq", query_vectors, fresh_keys, preferred_element_type=f32) * multiplier
    own = jnp.where(gx == 0, own, NEGATIVE)
    top = jnp.maximum(jnp.max(logits, axis=-1), own)
    weights = jnp.where(visible, jnp.exp(logits - top[..., None]), 0.0)
    own_weight = jnp.where(gx == 0, jnp.exp(own - top), 0.0)
    total = jnp.sum(weights, axis=-1) + own_weight
    scaled = (weights * value_scale[:, :, None, :]).astype(bf16)
    mixed = jnp.einsum("rgqs,rgsd->rgqd", scaled, value_cache, preferred_element_type=f32)
    mixed = mixed + own_weight[..., None] * fresh_values.astype(f32)[:, :, None, :]

    share = requests // n_gx
    mixed = mixed.reshape(n_gx, share * HEADS, HEAD_DIM)
    stats = jnp.concatenate([top.reshape(n_gx, share * HEADS // HEAD_DIM, HEAD_DIM),
                             total.reshape(n_gx, share * HEADS // HEAD_DIM, HEAD_DIM)], axis=1)
    extra = stats.shape[1]
    message = jnp.concatenate([mixed, stats, jnp.zeros((n_gx, -extra % 8, HEAD_DIM), f32)], axis=1)
    parts = exchange(message, "gx", n_gx)
    count = share * HEADS
    tops = [part[count : count + extra // 2].reshape(count) for part in parts]
    totals = [part[count + extra // 2 : count + extra].reshape(count) for part in parts]
    largest = tops[0]
    for other in tops[1:]:
        largest = jnp.maximum(largest, other)
    factors = [jnp.exp(t - largest) for t in tops]
    total = sum(f * t for f, t in zip(factors, totals))
    mixed = sum(f[:, None] * part[:count] for f, part in zip(factors, parts))
    attended = (mixed / total[:, None]).astype(bf16)
    attended = attended.reshape(share, n_gy, HEADS // n_gy * HEAD_DIM).transpose(1, 0, 2)
    blocks = jnp.stack(ordered(exchange(attended, "gy", n_gy), gy))
    blocks = jnp.stack(ordered(gather(blocks, "gx", n_gx), gx), axis=1)
    projected = jnp.dot(blocks.reshape(rows, -1), w_out, preferred_element_type=f32) * out_scale

    term = (projected + ffn_partial[0]).reshape(2, rows // 2, width)
    core = gy & 1
    kept = lax.dynamic_index_in_dim(term, core, 0, keepdims=False)
    given = lax.dynamic_index_in_dim(term, 1 - core, 0, keepdims=False)
    chip = kept + swap(given, "gy", n_gy, 1)
    whole = chip + swap(chip, "gy", n_gy, 2)
    half = lax.dynamic_slice_in_dim(widened, core * (rows // 2), rows // 2, 0)
    half = (half + whole).astype(bf16)
    return jnp.concatenate(ordered([half, swap(half, "gy", n_gy, 1)], core))


def joined(value, axis, join):
    pieces = jax.tree.map(lambda part: lax.all_gather(part, axis), value)
    head = jax.tree.map(lambda part: part[0], pieces)
    tail = jax.tree.map(lambda part: part[1:], pieces)
    subtotal, _ = lax.scan(lambda subtotal, piece: (join(subtotal, piece), None), head, tail)
    return subtotal


def combine(former, latter):
    top = jnp.maximum(former[0], latter[0])
    first_factor = jnp.exp(former[0] - top)
    second_factor = jnp.exp(latter[0] - top)
    total = former[1] * first_factor + latter[1] * second_factor
    mixed = former[2] * first_factor[..., None] + latter[2] * second_factor[..., None]
    return (top, total, mixed)


def plain_body(
    residual,
    ffn_partial,
    norm_gain,
    smooth_scale,
    w_query,
    query_scale,
    w_keyval,
    keyval_scale,
    key_cache,
    value_cache,
    key_scale,
    value_scale,
    lengths,
    w_out,
    out_scale,
):
    widened = residual.astype(jnp.float32)
    ffn_total = lax.psum(ffn_partial[0], "gy")
    squares = jnp.sum(widened * widened, axis=1)
    smoothed = (widened * (norm_gain / smooth_scale)).astype(jnp.bfloat16)
    query_part = jnp.dot(smoothed, w_query, preferred_element_type=jnp.float32) * query_scale
    keyval_part = jnp.dot(smoothed, w_keyval, preferred_element_type=jnp.float32) * keyval_scale
    query_sum, keyval_sum, square_sum = lax.psum((query_part, keyval_part, squares), "gx")
    row_scale = lax.rsqrt(square_sum / D + EPSILON)[:, None]
    query_rows = (row_scale * query_sum).astype(jnp.bfloat16)
    keyval_rows = (row_scale * keyval_sum).astype(jnp.bfloat16)
    query_vectors, keyvals = (
        lax.all_to_all(query_rows, "gy", split_axis=0, concat_axis=1, tiled=True),
        lax.all_to_all(keyval_rows, "gy", split_axis=0, concat_axis=1, tiled=True),
    )
    requests = query_vectors.shape[0]
    local = key_cache.shape[2]
    group = HEADS // KV_HEADS
    score_multiplier = HEAD_DIM ** (-0.5)
    grouped = query_vectors.reshape(requests, KV_HEADS, group, HEAD_DIM)
    fresh_key_rows = keyvals[:, : KV_HEADS * HEAD_DIM].reshape(requests, KV_HEADS, HEAD_DIM)
    fresh_value_rows = keyvals[:, KV_HEADS * HEAD_DIM :].reshape(requests, KV_HEADS, HEAD_DIM)
    logit_scores = jnp.einsum(
        "rgqd,rgsd->rgqs", grouped, key_cache, preferred_element_type=jnp.float32
    )
    logit_scores = logit_scores * key_scale[:, :, None, :] * score_multiplier
    position = lax.axis_index("gx") * local + jnp.arange(local, dtype=jnp.int32)
    visible = (position[None, :] < lengths[:, None])[:, None, None, :]
    logit_scores = jnp.where(visible, logit_scores, NEGATIVE)
    local_top = jnp.max(logit_scores, axis=-1)
    weights = jnp.where(visible, jnp.exp(logit_scores - local_top[..., None]), 0.0)
    local_total = jnp.sum(weights, axis=-1)
    scaled = (weights * value_scale[:, :, None, :]).astype(jnp.bfloat16)
    local_mixed = jnp.einsum(
        "rgqs,rgsd->rgqd", scaled, value_cache, preferred_element_type=jnp.float32
    )
    top, total, mixed = joined((local_top, local_total, local_mixed), "gx", combine)
    own = (
        jnp.einsum("rgqd,rgd->rgq", grouped, fresh_key_rows, preferred_element_type=jnp.float32)
        * score_multiplier
    )
    largest = jnp.maximum(top, own)
    old_factor = jnp.exp(top - largest)
    own_weight = jnp.exp(own - largest)
    total = total * old_factor + own_weight
    mixed = (
        mixed * old_factor[..., None]
        + own_weight[..., None] * fresh_value_rows.astype(jnp.float32)[:, :, None, :]
    )
    attended = (mixed / total[..., None]).astype(jnp.bfloat16).reshape(requests, HEADS * HEAD_DIM)
    head_block = lax.all_to_all(attended, "gy", split_axis=1, concat_axis=0, tiled=True)
    projected = jnp.dot(head_block, w_out, preferred_element_type=jnp.float32) * out_scale
    attention_total = lax.psum(projected, "gy")
    new_residual = (widened + ffn_total + attention_total).astype(jnp.bfloat16)
    return new_residual


def solution(mesh):
    placed = (
        P("rep", "gx"), P("gy", "rep", "gx"), P("gx"), P("gx"), P("gx", "gy"), P("gy"), P("gx", "gy"), P("gy"),
        P(("rep", "gy"), None, "gx", None), P(("rep", "gy"), None, "gx", None),
        P(("rep", "gy"), None, "gx"), P(("rep", "gy"), None, "gx"), P(("rep", "gy")), P("gy", "gx"), P("gx"),
    )
    n_gx, n_gy = mesh.shape["gx"], mesh.shape["gy"]

    def run(*arrays):
        if n_gx == 4 and n_gy == 4:
            return body(n_gx, n_gy, *arrays)
        return plain_body(*arrays)

    return jax.shard_map(run, mesh=mesh, in_specs=placed, out_specs=P("rep", "gx"), check_vma=False)
```

```python
import functools

import jax
import jax.numpy as jnp
from jax import lax
from jax.experimental import pallas as pl
from jax.experimental.pallas import tpu as pltpu
from jax.sharding import PartitionSpec as P

D = 16384
HEADS = 64
KV_HEADS = 4
HEAD_DIM = 128
GROUP = HEADS // KV_HEADS
EPSILON = 1e-05
NEGATIVE = -1e30
LANES = 128
f32 = jnp.float32
bf16 = jnp.bfloat16
VMEM = pl.BlockSpec(memory_space=pltpu.VMEM)
SMEM = pl.BlockSpec(memory_space=pltpu.SMEM)
ANY = pl.BlockSpec(memory_space=pl.ANY)


def partners(n, offset):
    return [(i, i ^ offset) for i in range(n)]


def ordered(pieces, me):
    n = len(pieces)
    return [lax.select_n(me, *[pieces[j ^ i] for i in range(n)]) for j in range(n)]


def trade(chunks, axis, n):
    return [chunks[0]] + [lax.ppermute(chunks[k], axis, partners(n, k)) for k in range(1, n)]


def gather(value, axis, n):
    return trade([value] * n, axis, n)


def swap(value, axis, n, offset):
    return lax.ppermute(value, axis, partners(n, offset))


def params(mib):
    return pltpu.CompilerParams(vmem_limit_bytes=mib << 20)


def project_kernel(n, residual, gain, smooth, w_query, query_scale, w_keyval, keyval_scale, *rest):
    outs = rest[:n]
    x_buf, g_buf, s_buf, q_buf, k_buf, qs_buf, ks_buf, smoothed, q_sum, k_sum, packed, sems, big_sems = rest[n:]
    rows, width = x_buf.shape
    steps = big_sems.shape[0] // 2
    depth = width // steps
    small = [
        pltpu.make_async_copy(source, target, sems.at[i])
        for i, (source, target) in enumerate(
            [(residual, x_buf), (gain, g_buf), (smooth, s_buf), (query_scale, qs_buf), (keyval_scale, ks_buf)]
        )
    ]
    for copy in small[:3]:
        copy.start()
    large = []
    for i in range(steps):
        part = pl.ds(i * depth, depth)
        large.append(
            (
                pltpu.make_async_copy(w_keyval.at[part], k_buf.at[part], big_sems.at[2 * i]),
                pltpu.make_async_copy(w_query.at[part], q_buf.at[part], big_sems.at[2 * i + 1]),
            )
        )
        for copy in large[-1]:
            copy.start()
    for copy in small[3:]:
        copy.start()
    for copy in small[:3]:
        copy.wait()
    squares = jnp.zeros((rows, LANES), f32)
    for i in range(width // LANES):
        lanes = slice(i * LANES, (i + 1) * LANES)
        x = x_buf[:, lanes].astype(f32)
        squares += x * x
        smoothed[:, lanes] = (x * (g_buf[i : i + 1, :] / s_buf[i : i + 1, :])).astype(bf16)
    squares = jnp.sum(squares, axis=1, keepdims=True)
    for i in range(steps):
        part = slice(i * depth, (i + 1) * depth)
        large[i][0].wait()
        k_part = jnp.dot(smoothed[:, part], k_buf[part, :], preferred_element_type=f32)
        large[i][1].wait()
        q_part = jnp.dot(smoothed[:, part], q_buf[part, :], preferred_element_type=f32)
        if i == 0:
            q_sum[...], k_sum[...] = q_part, k_part
        else:
            q_sum[...] += q_part
            k_sum[...] += k_part
    for copy in small[3:]:
        copy.wait()
    q_tiles = q_sum.shape[1] // LANES
    per = q_tiles // n
    for t in range(q_tiles):
        lanes = slice(t * LANES, (t + 1) * LANES)
        packed[t // per, :, (t % per) * LANES : (t % per + 1) * LANES] = q_sum[:, lanes] * qs_buf[t : t + 1, :]
    lane = lax.broadcasted_iota(jnp.int32, (rows, LANES), 1)
    half = k_sum.shape[1] // n
    for p in range(n):
        start = p * half
        t, shift = start // LANES, start % LANES
        tile = k_sum[:, t * LANES : (t + 1) * LANES] * ks_buf[t : t + 1, :]
        if shift:
            tile = pltpu.roll(tile, LANES - shift, 1)
        packed[p, :, per * LANES :] = jnp.where(lane < half, tile, squares)
    me = lax.axis_index("gx")
    for k in range(n):
        outs[k][...] = packed[me ^ k]


def project(n, residual, gain, smooth, w_query, query_scale, w_keyval, keyval_scale):
    rows, width = residual.shape
    queries, keyvals = w_query.shape[1], w_keyval.shape[1]
    columns = queries // n + LANES
    steps = 8
    return pl.pallas_call(
        functools.partial(project_kernel, n),
        in_specs=[ANY] * 7,
        out_specs=[VMEM] * n,
        out_shape=[jax.ShapeDtypeStruct((rows, columns), f32)] * n,
        scratch_shapes=[
            pltpu.VMEM((rows, width), bf16),
            pltpu.VMEM((width // LANES, LANES), f32),
            pltpu.VMEM((width // LANES, LANES), f32),
            pltpu.VMEM((width, queries), bf16),
            pltpu.VMEM((width, keyvals), bf16),
            pltpu.VMEM((queries // LANES, LANES), f32),
            pltpu.VMEM((keyvals // LANES, LANES), f32),
            pltpu.VMEM((rows, width), bf16),
            pltpu.VMEM((rows, queries), f32),
            pltpu.VMEM((rows, keyvals), f32),
            pltpu.VMEM((n, rows, columns), f32),
            pltpu.SemaphoreType.DMA((5,)),
            pltpu.SemaphoreType.DMA((2 * steps,)),
        ],
        compiler_params=params(50),
        name="project",
    )(
        residual,
        gain.reshape(-1, LANES),
        smooth.reshape(-1, LANES),
        w_query,
        query_scale.reshape(-1, LANES),
        w_keyval,
        keyval_scale.reshape(-1, LANES),
    )


def norm_kernel(n_gx, n_gy, half, *refs):
    parts, outs, full = refs[:n_gx], refs[n_gx : n_gx + n_gy], refs[-1]
    total = parts[0][...]
    for part in parts[1:]:
        total = total + part[...]
    columns = total.shape[1]
    squares = total[:, columns - LANES + half : columns - LANES + half + 1]
    full[...] = total * lax.rsqrt(squares / D + EPSILON)
    requests = total.shape[0] // n_gy
    me = lax.axis_index("gy")
    for k in range(n_gy):
        start = pl.multiple_of((me ^ k) * requests, requests)
        outs[k][...] = full[pl.ds(start, requests), :].astype(bf16)


def norm(n_gx, n_gy, half, parts):
    rows, columns = parts[0].shape
    return pl.pallas_call(
        functools.partial(norm_kernel, n_gx, n_gy, half),
        in_specs=[VMEM] * n_gx,
        out_specs=[VMEM] * n_gy,
        out_shape=[jax.ShapeDtypeStruct((rows // n_gy, columns), bf16)] * n_gy,
        scratch_shapes=[pltpu.VMEM((rows, columns), f32)],
        compiler_params=params(8),
        name="norm",
    )(*parts)


def attend_kernel(n, half, *refs):
    pieces = refs[:n]
    lengths, keys, values, key_scale, value_scale = refs[n : n + 5]
    outs = refs[n + 5 : 2 * n + 5]
    placed, k_buf, v_buf, q_rows, logits, messages, fresh, sems = refs[2 * n + 5 :]
    requests, _, local, _ = k_buf.shape
    load_keys = pltpu.make_async_copy(keys, k_buf, sems.at[0])
    load_values = pltpu.make_async_copy(values, v_buf, sems.at[1])
    load_keys.start()
    load_values.start()
    me = lax.axis_index("gx")
    for k in range(n):
        placed[me ^ k] = pieces[k][...].astype(f32)
    per = GROUP // n
    for g in range(KV_HEADS):
        for p in range(n):
            for j in range(per):
                tile = placed[p, g, :, j * LANES : (j + 1) * LANES]
                q_rows[pl.ds(g * GROUP + p * per + j, requests, stride=HEADS), :] = tile
    lane = lax.broadcasted_iota(jnp.int32, (requests, LANES), 1)
    tail = placed.shape[3] - LANES
    share = half * n
    for c in range(2 * KV_HEADS):
        block, start = c * LANES // share, c * LANES % share
        low = placed[start // half, block, :, tail:]
        high = placed[start // half + 1, block, :, tail:]
        fresh[pl.ds(c, requests, stride=2 * KV_HEADS), :] = jnp.where(lane < half, low, pltpu.roll(high, half, 1))
    multiplier = HEAD_DIM ** (-0.5)
    load_keys.wait()
    for r in range(requests):
        for g in range(KV_HEADS):
            at = slice(r * HEADS + g * GROUP, r * HEADS + (g + 1) * GROUP)
            logits[at, :] = lax.dot_general(
                q_rows[at, :].astype(bf16), k_buf[r, g], (((1,), (1,)), ((), ())), preferred_element_type=f32
            )
    load_values.wait()
    position = lax.broadcasted_iota(jnp.int32, (GROUP, local), 1) + me * local
    first = me == 0
    count = requests * HEADS // n
    tops, totals = [], []
    for r in range(requests):
        for g in range(KV_HEADS):
            row = r * HEADS + g * GROUP
            at = slice(row, row + GROUP)
            scale_at = r * KV_HEADS + g
            visible = position < lengths[r]
            scores = logits[at, :] * key_scale[scale_at : scale_at + 1, :] * multiplier
            scores = jnp.where(visible, scores, NEGATIVE)
            new_key = fresh[r * 2 * KV_HEADS + g : r * 2 * KV_HEADS + g + 1, :]
            new_value = fresh[r * 2 * KV_HEADS + KV_HEADS + g : r * 2 * KV_HEADS + KV_HEADS + g + 1, :]
            own = jnp.sum(q_rows[at, :] * new_key, axis=1, keepdims=True) * multiplier
            own = jnp.where(first, own, NEGATIVE)
            top = jnp.maximum(jnp.max(scores, axis=1, keepdims=True), own)
            weights = jnp.where(visible, jnp.exp(scores - top), 0.0)
            own_weight = jnp.where(first, jnp.exp(own - top), 0.0)
            totals.append(jnp.sum(weights, axis=1, keepdims=True) + own_weight)
            tops.append(top)
            scaled = (weights * value_scale[scale_at : scale_at + 1, :]).astype(bf16)
            mixed = jnp.dot(scaled, v_buf[r, g], preferred_element_type=f32) + own_weight * new_value
            messages[row // count, row % count : row % count + GROUP, :] = mixed
    diagonal = lax.broadcasted_iota(jnp.int32, (LANES, LANES), 0) == lax.broadcasted_iota(jnp.int32, (LANES, LANES), 1)
    step = count // GROUP
    wide = LANES // GROUP
    for p in range(n):
        rows = []
        for kind in (tops, totals):
            for b in range(count // LANES):
                column = jnp.concatenate(kind[p * step + b * wide : p * step + (b + 1) * wide], axis=0)
                rows.append(jnp.sum(jnp.where(diagonal, column, 0.0), axis=0, keepdims=True))
        spare = messages.shape[1] - count - len(rows)
        messages[p, count:, :] = jnp.concatenate(rows + [jnp.zeros((spare, LANES), f32)], axis=0)
    for k in range(n):
        outs[k][...] = messages[me ^ k]


def attend(n, half, pieces, lengths, keys, values, key_scale, value_scale):
    requests, _, local, _ = keys.shape
    count = requests * HEADS // n
    height = count + -(-2 * count // LANES // 8) * 8
    return pl.pallas_call(
        functools.partial(attend_kernel, n, half),
        in_specs=[VMEM] * n + [SMEM, ANY, ANY, VMEM, VMEM],
        out_specs=[VMEM] * n,
        out_shape=[jax.ShapeDtypeStruct((height, LANES), f32)] * n,
        scratch_shapes=[
            pltpu.VMEM((n,) + pieces[0].shape, f32),
            pltpu.VMEM(keys.shape, bf16),
            pltpu.VMEM(values.shape, bf16),
            pltpu.VMEM((requests * HEADS, HEAD_DIM), f32),
            pltpu.VMEM((requests * HEADS, local), f32),
            pltpu.VMEM((n, height, LANES), f32),
            pltpu.VMEM((requests * 2 * KV_HEADS, HEAD_DIM), f32),
            pltpu.SemaphoreType.DMA((2,)),
        ],
        compiler_params=params(32),
        name="attend",
    )(*pieces, lengths, keys, values, key_scale.reshape(-1, local), value_scale.reshape(-1, local))


def output_kernel(attended, w_out, out_scale, ffn, kept, given, w_buf, ffn_buf, total, sems):
    depth_all, width = w_buf.shape
    steps = sems.shape[0] - 1
    depth = depth_all // steps
    copies = []
    for i in range(steps):
        part = pl.ds(i * depth, depth)
        copies.append(pltpu.make_async_copy(w_out.at[part], w_buf.at[part], sems.at[i]))
        copies[-1].start()
    load = pltpu.make_async_copy(ffn, ffn_buf, sems.at[steps])
    load.start()
    for i in range(steps):
        part = slice(i * depth, (i + 1) * depth)
        copies[i].wait()
        term = jnp.dot(attended[:, part], w_buf[part, :], preferred_element_type=f32)
        if i == 0:
            total[...] = term
        else:
            total[...] += term
    load.wait()
    for t in range(width // LANES):
        lanes = slice(t * LANES, (t + 1) * LANES)
        total[:, lanes] = total[:, lanes] * out_scale[t : t + 1, :] + ffn_buf[:, lanes]
    rows = total.shape[0] // 2
    core = lax.axis_index("gy") & 1
    kept[...] = total[pl.ds(pl.multiple_of(core * rows, rows), rows), :]
    given[...] = total[pl.ds(pl.multiple_of((1 - core) * rows, rows), rows), :]


def output(attended, w_out, out_scale, ffn):
    rows, depth = attended.shape
    width = w_out.shape[1]
    steps = 8
    return pl.pallas_call(
        output_kernel,
        in_specs=[VMEM, ANY, VMEM, ANY],
        out_specs=[VMEM] * 2,
        out_shape=[jax.ShapeDtypeStruct((rows // 2, width), f32)] * 2,
        scratch_shapes=[
            pltpu.VMEM(w_out.shape, bf16),
            pltpu.VMEM((rows, width), f32),
            pltpu.VMEM((rows, width), f32),
            pltpu.SemaphoreType.DMA((steps + 1,)),
        ],
        compiler_params=params(50),
        name="output",
    )(attended, w_out, out_scale.reshape(-1, LANES), ffn)


def body(n_gx, n_gy, residual, ffn_partial, norm_gain, smooth_scale, w_query, query_scale, w_keyval, keyval_scale,
         key_cache, value_cache, key_scale, value_scale, lengths, w_out, out_scale):
    gx, gy = lax.axis_index("gx"), lax.axis_index("gy")
    rows, width = residual.shape
    half = w_keyval.shape[1] // n_gx
    parts = project(n_gx, residual, norm_gain, smooth_scale, w_query, query_scale, w_keyval, keyval_scale)
    parts = trade(parts, "gx", n_gx)
    blocks = trade(norm(n_gx, n_gy, half, parts), "gy", n_gy)
    mine = jnp.stack(ordered(blocks, gy))
    pieces = gather(mine, "gx", n_gx)
    parts = attend(n_gx, half, pieces, lengths, key_cache, value_cache, key_scale, value_scale)
    parts = trade(parts, "gx", n_gx)

    share = rows // n_gy // n_gx
    count = share * HEADS
    extra = 2 * count // LANES
    tops = [part[count : count + extra // 2].reshape(count) for part in parts]
    totals = [part[count + extra // 2 : count + extra].reshape(count) for part in parts]
    largest = tops[0]
    for other in tops[1:]:
        largest = jnp.maximum(largest, other)
    factors = [jnp.exp(t - largest) for t in tops]
    total = sum(f * t for f, t in zip(factors, totals))
    mixed = sum(f[:, None] * part[:count] for f, part in zip(factors, parts))
    attended = (mixed / total[:, None]).astype(bf16)
    attended = attended.reshape(share, n_gy, HEADS // n_gy * HEAD_DIM).transpose(1, 0, 2)
    sends = [lax.dynamic_index_in_dim(attended, gy ^ k, 0, keepdims=False) for k in range(n_gy)]
    blocks = jnp.stack(ordered(trade(sends, "gy", n_gy), gy))
    blocks = jnp.stack(ordered(gather(blocks, "gx", n_gx), gx), axis=1)
    kept, given = output(blocks.reshape(rows, -1), w_out, out_scale, ffn_partial[0])
    core = gy & 1
    chip = kept + swap(given, "gy", n_gy, 1)
    whole = chip + swap(chip, "gy", n_gy, 2)
    mine = lax.dynamic_slice_in_dim(residual, core * (rows // 2), rows // 2, 0)
    mine = (mine.astype(f32) + whole).astype(bf16)
    return jnp.concatenate(ordered([mine, swap(mine, "gy", n_gy, 1)], core))


def joined(value, axis, join):
    pieces = jax.tree.map(lambda part: lax.all_gather(part, axis), value)
    head = jax.tree.map(lambda part: part[0], pieces)
    tail = jax.tree.map(lambda part: part[1:], pieces)
    subtotal, _ = lax.scan(lambda subtotal, piece: (join(subtotal, piece), None), head, tail)
    return subtotal


def combine(former, latter):
    top = jnp.maximum(former[0], latter[0])
    first_factor = jnp.exp(former[0] - top)
    second_factor = jnp.exp(latter[0] - top)
    total = former[1] * first_factor + latter[1] * second_factor
    mixed = former[2] * first_factor[..., None] + latter[2] * second_factor[..., None]
    return (top, total, mixed)


def plain_body(
    residual,
    ffn_partial,
    norm_gain,
    smooth_scale,
    w_query,
    query_scale,
    w_keyval,
    keyval_scale,
    key_cache,
    value_cache,
    key_scale,
    value_scale,
    lengths,
    w_out,
    out_scale,
):
    widened = residual.astype(jnp.float32)
    ffn_total = lax.psum(ffn_partial[0], "gy")
    squares = jnp.sum(widened * widened, axis=1)
    smoothed = (widened * (norm_gain / smooth_scale)).astype(jnp.bfloat16)
    query_part = jnp.dot(smoothed, w_query, preferred_element_type=jnp.float32) * query_scale
    keyval_part = jnp.dot(smoothed, w_keyval, preferred_element_type=jnp.float32) * keyval_scale
    query_sum, keyval_sum, square_sum = lax.psum((query_part, keyval_part, squares), "gx")
    row_scale = lax.rsqrt(square_sum / D + EPSILON)[:, None]
    query_rows = (row_scale * query_sum).astype(jnp.bfloat16)
    keyval_rows = (row_scale * keyval_sum).astype(jnp.bfloat16)
    query_vectors, keyvals = (
        lax.all_to_all(query_rows, "gy", split_axis=0, concat_axis=1, tiled=True),
        lax.all_to_all(keyval_rows, "gy", split_axis=0, concat_axis=1, tiled=True),
    )
    requests = query_vectors.shape[0]
    local = key_cache.shape[2]
    group = HEADS // KV_HEADS
    score_multiplier = HEAD_DIM ** (-0.5)
    grouped = query_vectors.reshape(requests, KV_HEADS, group, HEAD_DIM)
    fresh_key_rows = keyvals[:, : KV_HEADS * HEAD_DIM].reshape(requests, KV_HEADS, HEAD_DIM)
    fresh_value_rows = keyvals[:, KV_HEADS * HEAD_DIM :].reshape(requests, KV_HEADS, HEAD_DIM)
    logit_scores = jnp.einsum(
        "rgqd,rgsd->rgqs", grouped, key_cache, preferred_element_type=jnp.float32
    )
    logit_scores = logit_scores * key_scale[:, :, None, :] * score_multiplier
    position = lax.axis_index("gx") * local + jnp.arange(local, dtype=jnp.int32)
    visible = (position[None, :] < lengths[:, None])[:, None, None, :]
    logit_scores = jnp.where(visible, logit_scores, NEGATIVE)
    local_top = jnp.max(logit_scores, axis=-1)
    weights = jnp.where(visible, jnp.exp(logit_scores - local_top[..., None]), 0.0)
    local_total = jnp.sum(weights, axis=-1)
    scaled = (weights * value_scale[:, :, None, :]).astype(jnp.bfloat16)
    local_mixed = jnp.einsum(
        "rgqs,rgsd->rgqd", scaled, value_cache, preferred_element_type=jnp.float32
    )
    top, total, mixed = joined((local_top, local_total, local_mixed), "gx", combine)
    own = (
        jnp.einsum("rgqd,rgd->rgq", grouped, fresh_key_rows, preferred_element_type=jnp.float32)
        * score_multiplier
    )
    largest = jnp.maximum(top, own)
    old_factor = jnp.exp(top - largest)
    own_weight = jnp.exp(own - largest)
    total = total * old_factor + own_weight
    mixed = (
        mixed * old_factor[..., None]
        + own_weight[..., None] * fresh_value_rows.astype(jnp.float32)[:, :, None, :]
    )
    attended = (mixed / total[..., None]).astype(jnp.bfloat16).reshape(requests, HEADS * HEAD_DIM)
    head_block = lax.all_to_all(attended, "gy", split_axis=1, concat_axis=0, tiled=True)
    projected = jnp.dot(head_block, w_out, preferred_element_type=jnp.float32) * out_scale
    attention_total = lax.psum(projected, "gy")
    new_residual = (widened + ffn_total + attention_total).astype(jnp.bfloat16)
    return new_residual


def solution(mesh):
    placed = (
        P("rep", "gx"), P("gy", "rep", "gx"), P("gx"), P("gx"), P("gx", "gy"), P("gy"), P("gx", "gy"), P("gy"),
        P(("rep", "gy"), None, "gx", None), P(("rep", "gy"), None, "gx", None),
        P(("rep", "gy"), None, "gx"), P(("rep", "gy"), None, "gx"), P(("rep", "gy")), P("gy", "gx"), P("gx"),
    )
    n_gx, n_gy = mesh.shape["gx"], mesh.shape["gy"]

    def run(*arrays):
        if n_gx == 4 and n_gy == 4:
            return body(n_gx, n_gy, *arrays)
        return plain_body(*arrays)

    return jax.shard_map(run, mesh=mesh, in_specs=placed, out_specs=P("rep", "gx"), check_vma=False)
```

```python
import functools

import jax
import jax.numpy as jnp
from jax import lax
from jax.experimental import pallas as pl
from jax.experimental.pallas import tpu as pltpu
from jax.sharding import PartitionSpec as P

D = 16384
HEADS = 64
KV_HEADS = 4
HEAD_DIM = 128
GROUP = HEADS // KV_HEADS
EPSILON = 1e-05
NEGATIVE = -1e30
LANES = 128
f32 = jnp.float32
bf16 = jnp.bfloat16
VMEM = pl.BlockSpec(memory_space=pltpu.VMEM)
SMEM = pl.BlockSpec(memory_space=pltpu.SMEM)
ANY = pl.BlockSpec(memory_space=pl.ANY)
HBM = pl.BlockSpec(memory_space=pltpu.HBM)


def partners(n, offset):
    return [(i, i ^ offset) for i in range(n)]


def ordered(pieces, me):
    n = len(pieces)
    return [lax.select_n(me, *[pieces[j ^ i] for i in range(n)]) for j in range(n)]


def trade(chunks, axis, n):
    return [chunks[0]] + [lax.ppermute(chunks[k], axis, partners(n, k)) for k in range(1, n)]


def spread(value, n):
    return [
        lax.ppermute(value, ("gx", "gy"), [(a * n + b, (b ^ k) * n + a) for a in range(n) for b in range(n)])
        for k in range(n)
    ]


def swap(value, axis, n, offset):
    return lax.ppermute(value, axis, partners(n, offset))


def params(mib):
    return pltpu.CompilerParams(vmem_limit_bytes=mib << 20)


def project_kernel(n, residual, gain, smooth, w_query, query_scale, w_keyval, keyval_scale, *rest):
    outs = rest[:n]
    x_buf, g_buf, s_buf, q_buf, k_buf, qs_buf, ks_buf, smoothed, q_sum, k_sum, squares_sum, sems, big_sems = rest[n:]
    rows, width = x_buf.shape
    steps = big_sems.shape[0] // 2
    depth = width // steps
    small = [
        pltpu.make_async_copy(source, target, sems.at[i])
        for i, (source, target) in enumerate(
            [(residual, x_buf), (gain, g_buf), (smooth, s_buf), (query_scale, qs_buf), (keyval_scale, ks_buf)]
        )
    ]
    for copy in small[:3]:
        copy.start()
    large = []
    for i in range(steps):
        part = pl.ds(i * depth, depth)
        large.append(
            (
                pltpu.make_async_copy(w_keyval.at[part], k_buf.at[part], big_sems.at[2 * i]),
                pltpu.make_async_copy(w_query.at[part], q_buf.at[part], big_sems.at[2 * i + 1]),
            )
        )
        for copy in large[-1]:
            copy.start()
    for copy in small[3:]:
        copy.start()
    for copy in small[:3]:
        copy.wait()
    squares = jnp.zeros((rows, LANES), f32)
    for i in range(width // LANES):
        lanes = slice(i * LANES, (i + 1) * LANES)
        x = x_buf[:, lanes].astype(f32)
        squares += x * x
        smoothed[:, lanes] = (x * (g_buf[i : i + 1, :] / s_buf[i : i + 1, :])).astype(bf16)
    squares = jnp.sum(squares, axis=1, keepdims=True)
    for i in range(steps):
        part = slice(i * depth, (i + 1) * depth)
        large[i][0].wait()
        k_part = jnp.dot(smoothed[:, part], k_buf[part, :], preferred_element_type=f32)
        large[i][1].wait()
        q_part = jnp.dot(smoothed[:, part], q_buf[part, :], preferred_element_type=f32)
        if i == 0:
            q_sum[...], k_sum[...] = q_part, k_part
        else:
            q_sum[...] += q_part
            k_sum[...] += k_part
    for copy in small[3:]:
        copy.wait()
    me = lax.axis_index("gx")
    requests = rows // n
    q_tiles, k_tiles = q_sum.shape[1] // LANES, k_sum.shape[1] // LANES
    squares_sum[...] = jnp.broadcast_to(squares, (rows, LANES))
    for k in range(n):
        at = pl.ds(pl.multiple_of((me ^ k) * requests, requests), requests)
        for t in range(q_tiles):
            lanes = slice(t * LANES, (t + 1) * LANES)
            outs[k][:, lanes] = q_sum[at, lanes] * qs_buf[t : t + 1, :]
        for t in range(k_tiles):
            lanes = slice(t * LANES, (t + 1) * LANES)
            outs[k][:, (q_tiles + t) * LANES : (q_tiles + t + 1) * LANES] = k_sum[at, lanes] * ks_buf[t : t + 1, :]
        outs[k][:, (q_tiles + k_tiles) * LANES :] = squares_sum[at, :]


def project(n, residual, gain, smooth, w_query, query_scale, w_keyval, keyval_scale):
    rows, width = residual.shape
    queries, keyvals = w_query.shape[1], w_keyval.shape[1]
    columns = queries + keyvals + LANES
    steps = 8
    return pl.pallas_call(
        functools.partial(project_kernel, n),
        in_specs=[HBM] * 7,
        out_specs=[VMEM] * n,
        out_shape=[jax.ShapeDtypeStruct((rows // n, columns), f32)] * n,
        scratch_shapes=[
            pltpu.VMEM((rows, width), bf16),
            pltpu.VMEM((width // LANES, LANES), f32),
            pltpu.VMEM((width // LANES, LANES), f32),
            pltpu.VMEM((width, queries), bf16),
            pltpu.VMEM((width, keyvals), bf16),
            pltpu.VMEM((queries // LANES, LANES), f32),
            pltpu.VMEM((keyvals // LANES, LANES), f32),
            pltpu.VMEM((rows, width), bf16),
            pltpu.VMEM((rows, queries), f32),
            pltpu.VMEM((rows, keyvals), f32),
            pltpu.VMEM((rows, LANES), f32),
            pltpu.SemaphoreType.DMA((5,)),
            pltpu.SemaphoreType.DMA((2 * steps,)),
        ],
        compiler_params=params(50),
        name="project",
    )(
        residual,
        gain.reshape(-1, LANES),
        smooth.reshape(-1, LANES),
        w_query,
        query_scale.reshape(-1, LANES),
        w_keyval,
        keyval_scale.reshape(-1, LANES),
    )


def norm_kernel(*refs):
    parts, out = refs[:-1], refs[-1]
    total = parts[0][...]
    for part in parts[1:]:
        total = total + part[...]
    columns = out.shape[1]
    out[...] = (total[:, :columns] * lax.rsqrt(total[:, columns : columns + 1] / D + EPSILON)).astype(bf16)


def norm(parts):
    rows, columns = parts[0].shape
    return pl.pallas_call(
        norm_kernel,
        in_specs=[VMEM] * len(parts),
        out_specs=VMEM,
        out_shape=jax.ShapeDtypeStruct((rows, columns - LANES), bf16),
        compiler_params=params(8),
        name="norm",
    )(*parts)


def attend_kernel(n, *refs):
    pieces = refs[:n]
    lengths, keys, values, key_scale, value_scale = refs[n : n + 5]
    outs = refs[n + 5 : 2 * n + 5]
    placed, k_buf, v_buf, q_rows, logits, messages, fresh, sems = refs[2 * n + 5 :]
    requests, _, local, _ = k_buf.shape
    load_keys = pltpu.make_async_copy(keys, k_buf, sems.at[0])
    load_values = pltpu.make_async_copy(values, v_buf, sems.at[1])
    load_keys.start()
    load_values.start()
    me = lax.axis_index("gx")
    for k in range(n):
        placed[me ^ k] = pieces[k][...].astype(f32)
    queries = HEADS * HEAD_DIM // n
    per = queries // LANES
    for h in range(HEADS):
        tile = placed[h // per, :, (h % per) * LANES : (h % per + 1) * LANES]
        q_rows[pl.ds(h, requests, stride=HEADS), :] = tile
    share = (placed.shape[2] - queries) // LANES
    for c in range(2 * KV_HEADS):
        start = queries + c % share * LANES
        fresh[pl.ds(c, requests, stride=2 * KV_HEADS), :] = placed[c // share, :, start : start + LANES]
    multiplier = HEAD_DIM ** (-0.5)
    load_keys.wait()
    for r in range(requests):
        for g in range(KV_HEADS):
            at = slice(r * HEADS + g * GROUP, r * HEADS + (g + 1) * GROUP)
            logits[at, :] = lax.dot_general(
                q_rows[at, :].astype(bf16), k_buf[r, g], (((1,), (1,)), ((), ())), preferred_element_type=f32
            )
    load_values.wait()
    position = lax.broadcasted_iota(jnp.int32, (GROUP, local), 1) + me * local
    first = me == 0
    count = requests * GROUP
    tops, totals = [[] for _ in range(n)], [[] for _ in range(n)]
    for r in range(requests):
        for g in range(KV_HEADS):
            row = r * HEADS + g * GROUP
            at = slice(row, row + GROUP)
            scale_at = r * KV_HEADS + g
            visible = position < lengths[r]
            scores = logits[at, :] * key_scale[scale_at : scale_at + 1, :] * multiplier
            scores = jnp.where(visible, scores, NEGATIVE)
            new_key = fresh[r * 2 * KV_HEADS + g : r * 2 * KV_HEADS + g + 1, :]
            new_value = fresh[r * 2 * KV_HEADS + KV_HEADS + g : r * 2 * KV_HEADS + KV_HEADS + g + 1, :]
            own = jnp.sum(q_rows[at, :] * new_key, axis=1, keepdims=True) * multiplier
            own = jnp.where(first, own, NEGATIVE)
            top = jnp.maximum(jnp.max(scores, axis=1, keepdims=True), own)
            weights = jnp.where(visible, jnp.exp(scores - top), 0.0)
            own_weight = jnp.where(first, jnp.exp(own - top), 0.0)
            totals[g].append(jnp.sum(weights, axis=1, keepdims=True) + own_weight)
            tops[g].append(top)
            scaled = (weights * value_scale[scale_at : scale_at + 1, :]).astype(bf16)
            mixed = jnp.dot(scaled, v_buf[r, g], preferred_element_type=f32) + own_weight * new_value
            messages[g, r * GROUP : (r + 1) * GROUP, :] = mixed
    diagonal = lax.broadcasted_iota(jnp.int32, (LANES, LANES), 0) == lax.broadcasted_iota(jnp.int32, (LANES, LANES), 1)
    wide = LANES // GROUP
    for p in range(n):
        rows = []
        for kind in (tops, totals):
            for b in range(count // LANES):
                column = jnp.concatenate(kind[p][b * wide : (b + 1) * wide], axis=0)
                rows.append(jnp.sum(jnp.where(diagonal, column, 0.0), axis=0, keepdims=True))
        spare = messages.shape[1] - count - len(rows)
        messages[p, count:, :] = jnp.concatenate(rows + [jnp.zeros((spare, LANES), f32)], axis=0)
    for k in range(n):
        outs[k][...] = messages[me ^ k]


def attend(n, pieces, lengths, keys, values, key_scale, value_scale):
    requests, _, local, _ = keys.shape
    count = requests * GROUP
    height = count + -(-2 * count // LANES // 8) * 8
    return pl.pallas_call(
        functools.partial(attend_kernel, n),
        in_specs=[VMEM] * n + [SMEM, ANY, ANY, VMEM, VMEM],
        out_specs=[VMEM] * n,
        out_shape=[jax.ShapeDtypeStruct((height, LANES), f32)] * n,
        scratch_shapes=[
            pltpu.VMEM((n,) + pieces[0].shape, f32),
            pltpu.VMEM(keys.shape, bf16),
            pltpu.VMEM(values.shape, bf16),
            pltpu.VMEM((requests * HEADS, HEAD_DIM), f32),
            pltpu.VMEM((requests * HEADS, local), f32),
            pltpu.VMEM((n, height, LANES), f32),
            pltpu.VMEM((requests * 2 * KV_HEADS, HEAD_DIM), f32),
            pltpu.SemaphoreType.DMA((2,)),
        ],
        compiler_params=params(32),
        name="attend",
    )(*pieces, lengths, keys, values, key_scale.reshape(-1, local), value_scale.reshape(-1, local))


def merge_kernel(*refs):
    parts, out, mixed = refs[:-2], refs[-2], refs[-1]
    count = mixed.shape[0]
    requests = out.shape[0]
    diagonal = lax.broadcasted_iota(jnp.int32, (LANES, LANES), 0) == lax.broadcasted_iota(jnp.int32, (LANES, LANES), 1)
    blocks = count // LANES
    for b in range(blocks):
        at = slice(b * LANES, (b + 1) * LANES)
        tops = [part[count + b : count + b + 1, :] for part in parts]
        totals = [part[count + blocks + b : count + blocks + b + 1, :] for part in parts]
        largest = tops[0]
        for top in tops[1:]:
            largest = jnp.maximum(largest, top)
        factors = [jnp.exp(top - largest) for top in tops]
        total = factors[0] * totals[0]
        for factor, other in zip(factors[1:], totals[1:]):
            total = total + factor * other
        sums = None
        for factor, part in zip(factors, parts):
            column = jnp.sum(jnp.where(diagonal, factor, 0.0), axis=1, keepdims=True)
            term = column * part[at, :]
            sums = term if sums is None else sums + term
        column = jnp.sum(jnp.where(diagonal, total, 0.0), axis=1, keepdims=True)
        mixed[at, :] = sums / column
    for h in range(count // requests):
        out[:, h * HEAD_DIM : (h + 1) * HEAD_DIM] = mixed[pl.ds(h, requests, stride=count // requests), :].astype(bf16)


def merge(parts, requests):
    count = requests * GROUP
    return pl.pallas_call(
        merge_kernel,
        in_specs=[VMEM] * len(parts),
        out_specs=VMEM,
        out_shape=jax.ShapeDtypeStruct((requests, GROUP * HEAD_DIM), bf16),
        scratch_shapes=[pltpu.VMEM((count, HEAD_DIM), f32)],
        compiler_params=params(8),
        name="merge",
    )(*parts)


def output_kernel(n, *refs):
    pieces = refs[:n]
    w_out, out_scale, ffn, kept, given, w_buf, ffn_buf, total, placed, sems = refs[n:]
    depth_all, width = w_buf.shape
    steps = sems.shape[0] - 1
    depth = depth_all // steps
    copies = []
    for i in range(steps):
        part = pl.ds(i * depth, depth)
        copies.append(pltpu.make_async_copy(w_out.at[part], w_buf.at[part], sems.at[i]))
        copies[-1].start()
    load = pltpu.make_async_copy(ffn, ffn_buf, sems.at[steps])
    load.start()
    me = lax.axis_index("gx")
    for k in range(n):
        placed[me ^ k] = pieces[k][...].astype(f32)
    for i in range(steps):
        part = slice(i * depth, (i + 1) * depth)
        copies[i].wait()
        attended = placed[:, :, part].reshape(total.shape[0], depth).astype(bf16)
        term = jnp.dot(attended, w_buf[part, :], preferred_element_type=f32)
        if i == 0:
            total[...] = term
        else:
            total[...] += term
    load.wait()
    for t in range(width // LANES):
        lanes = slice(t * LANES, (t + 1) * LANES)
        total[:, lanes] = total[:, lanes] * out_scale[t : t + 1, :] + ffn_buf[:, lanes]
    rows = total.shape[0] // 2
    core = lax.axis_index("gy") & 1
    kept[...] = total[pl.ds(pl.multiple_of(core * rows, rows), rows), :]
    given[...] = total[pl.ds(pl.multiple_of((1 - core) * rows, rows), rows), :]


def output(pieces, w_out, out_scale, ffn):
    n = len(pieces)
    rows = ffn.shape[0]
    width = w_out.shape[1]
    steps = 8
    return pl.pallas_call(
        functools.partial(output_kernel, n),
        in_specs=[VMEM] * n + [HBM, VMEM, HBM],
        out_specs=[VMEM] * 2,
        out_shape=[jax.ShapeDtypeStruct((rows // 2, width), f32)] * 2,
        scratch_shapes=[
            pltpu.VMEM(w_out.shape, bf16),
            pltpu.VMEM((rows, width), f32),
            pltpu.VMEM((rows, width), f32),
            pltpu.VMEM((n,) + pieces[0].shape, f32),
            pltpu.SemaphoreType.DMA((steps + 1,)),
        ],
        compiler_params=params(50),
        name="output",
    )(*pieces, w_out, out_scale.reshape(-1, LANES), ffn)


def body(n_gx, n_gy, residual, ffn_partial, norm_gain, smooth_scale, w_query, query_scale, w_keyval, keyval_scale,
         key_cache, value_cache, key_scale, value_scale, lengths, w_out, out_scale):
    gy = lax.axis_index("gy")
    rows = residual.shape[0]
    requests = rows // n_gy
    parts = project(n_gx, residual, norm_gain, smooth_scale, w_query, query_scale, w_keyval, keyval_scale)
    pieces = spread(norm(trade(parts, "gx", n_gx)), n_gx)
    parts = attend(n_gx, pieces, lengths, key_cache, value_cache, key_scale, value_scale)
    pieces = spread(merge(trade(parts, "gx", n_gx), requests), n_gx)
    kept, given = output(pieces, w_out, out_scale, ffn_partial[0])
    core = gy & 1
    chip = kept + swap(given, "gy", n_gy, 1)
    whole = chip + swap(chip, "gy", n_gy, 2)
    mine = lax.dynamic_slice_in_dim(residual, core * (rows // 2), rows // 2, 0)
    mine = (mine.astype(f32) + whole).astype(bf16)
    return jnp.concatenate(ordered([mine, swap(mine, "gy", n_gy, 1)], core))


def joined(value, axis, join):
    pieces = jax.tree.map(lambda part: lax.all_gather(part, axis), value)
    head = jax.tree.map(lambda part: part[0], pieces)
    tail = jax.tree.map(lambda part: part[1:], pieces)
    subtotal, _ = lax.scan(lambda subtotal, piece: (join(subtotal, piece), None), head, tail)
    return subtotal


def combine(former, latter):
    top = jnp.maximum(former[0], latter[0])
    first_factor = jnp.exp(former[0] - top)
    second_factor = jnp.exp(latter[0] - top)
    total = former[1] * first_factor + latter[1] * second_factor
    mixed = former[2] * first_factor[..., None] + latter[2] * second_factor[..., None]
    return (top, total, mixed)


def plain_body(
    residual,
    ffn_partial,
    norm_gain,
    smooth_scale,
    w_query,
    query_scale,
    w_keyval,
    keyval_scale,
    key_cache,
    value_cache,
    key_scale,
    value_scale,
    lengths,
    w_out,
    out_scale,
):
    widened = residual.astype(jnp.float32)
    ffn_total = lax.psum(ffn_partial[0], "gy")
    squares = jnp.sum(widened * widened, axis=1)
    smoothed = (widened * (norm_gain / smooth_scale)).astype(jnp.bfloat16)
    query_part = jnp.dot(smoothed, w_query, preferred_element_type=jnp.float32) * query_scale
    keyval_part = jnp.dot(smoothed, w_keyval, preferred_element_type=jnp.float32) * keyval_scale
    query_sum, keyval_sum, square_sum = lax.psum((query_part, keyval_part, squares), "gx")
    row_scale = lax.rsqrt(square_sum / D + EPSILON)[:, None]
    query_rows = (row_scale * query_sum).astype(jnp.bfloat16)
    keyval_rows = (row_scale * keyval_sum).astype(jnp.bfloat16)
    query_vectors, keyvals = (
        lax.all_to_all(query_rows, "gy", split_axis=0, concat_axis=1, tiled=True),
        lax.all_to_all(keyval_rows, "gy", split_axis=0, concat_axis=1, tiled=True),
    )
    requests = query_vectors.shape[0]
    local = key_cache.shape[2]
    group = HEADS // KV_HEADS
    score_multiplier = HEAD_DIM ** (-0.5)
    grouped = query_vectors.reshape(requests, KV_HEADS, group, HEAD_DIM)
    fresh_key_rows = keyvals[:, : KV_HEADS * HEAD_DIM].reshape(requests, KV_HEADS, HEAD_DIM)
    fresh_value_rows = keyvals[:, KV_HEADS * HEAD_DIM :].reshape(requests, KV_HEADS, HEAD_DIM)
    logit_scores = jnp.einsum(
        "rgqd,rgsd->rgqs", grouped, key_cache, preferred_element_type=jnp.float32
    )
    logit_scores = logit_scores * key_scale[:, :, None, :] * score_multiplier
    position = lax.axis_index("gx") * local + jnp.arange(local, dtype=jnp.int32)
    visible = (position[None, :] < lengths[:, None])[:, None, None, :]
    logit_scores = jnp.where(visible, logit_scores, NEGATIVE)
    local_top = jnp.max(logit_scores, axis=-1)
    weights = jnp.where(visible, jnp.exp(logit_scores - local_top[..., None]), 0.0)
    local_total = jnp.sum(weights, axis=-1)
    scaled = (weights * value_scale[:, :, None, :]).astype(jnp.bfloat16)
    local_mixed = jnp.einsum(
        "rgqs,rgsd->rgqd", scaled, value_cache, preferred_element_type=jnp.float32
    )
    top, total, mixed = joined((local_top, local_total, local_mixed), "gx", combine)
    own = (
        jnp.einsum("rgqd,rgd->rgq", grouped, fresh_key_rows, preferred_element_type=jnp.float32)
        * score_multiplier
    )
    largest = jnp.maximum(top, own)
    old_factor = jnp.exp(top - largest)
    own_weight = jnp.exp(own - largest)
    total = total * old_factor + own_weight
    mixed = (
        mixed * old_factor[..., None]
        + own_weight[..., None] * fresh_value_rows.astype(jnp.float32)[:, :, None, :]
    )
    attended = (mixed / total[..., None]).astype(jnp.bfloat16).reshape(requests, HEADS * HEAD_DIM)
    head_block = lax.all_to_all(attended, "gy", split_axis=1, concat_axis=0, tiled=True)
    projected = jnp.dot(head_block, w_out, preferred_element_type=jnp.float32) * out_scale
    attention_total = lax.psum(projected, "gy")
    new_residual = (widened + ffn_total + attention_total).astype(jnp.bfloat16)
    return new_residual


def solution(mesh):
    placed = (
        P("rep", "gx"), P("gy", "rep", "gx"), P("gx"), P("gx"), P("gx", "gy"), P("gy"), P("gx", "gy"), P("gy"),
        P(("rep", "gy"), None, "gx", None), P(("rep", "gy"), None, "gx", None),
        P(("rep", "gy"), None, "gx"), P(("rep", "gy"), None, "gx"), P(("rep", "gy")), P("gy", "gx"), P("gx"),
    )
    n_gx, n_gy = mesh.shape["gx"], mesh.shape["gy"]

    def run(*arrays):
        if n_gx == 4 and n_gy == 4:
            return body(n_gx, n_gy, *arrays)
        return plain_body(*arrays)

    return jax.shard_map(run, mesh=mesh, in_specs=placed, out_specs=P("rep", "gx"), check_vma=False)
```

```python
import functools

import jax
import jax.numpy as jnp
from jax import lax
from jax.experimental import pallas as pl
from jax.experimental.pallas import tpu as pltpu
from jax.sharding import PartitionSpec as P

D = 16384
HEADS = 64
KV_HEADS = 4
HEAD_DIM = 128
GROUP = HEADS // KV_HEADS
EPSILON = 1e-05
NEGATIVE = -1e30
LANES = 128
f32 = jnp.float32
bf16 = jnp.bfloat16
VMEM = pl.BlockSpec(memory_space=pltpu.VMEM)
SMEM = pl.BlockSpec(memory_space=pltpu.SMEM)
ANY = pl.BlockSpec(memory_space=pl.ANY)
HBM = pl.BlockSpec(memory_space=pltpu.HBM)


def partners(n, offset):
    return [(i, i ^ offset) for i in range(n)]


def ordered(pieces, me):
    n = len(pieces)
    return [lax.select_n(me, *[pieces[j ^ i] for i in range(n)]) for j in range(n)]


def trade(chunks, axis, n):
    return [chunks[0]] + [lax.ppermute(chunks[k], axis, partners(n, k)) for k in range(1, n)]


def spread(value, n):
    return [
        lax.ppermute(value, ("gx", "gy"), [(a * n + b, (b ^ k) * n + a) for a in range(n) for b in range(n)])
        for k in range(n)
    ]


def swap(value, axis, n, offset):
    return lax.ppermute(value, axis, partners(n, offset))


def params(mib):
    return pltpu.CompilerParams(vmem_limit_bytes=mib << 20)


def project_kernel(n, residual, gain, smooth, w_query, w_keyval, *rest):
    outs = rest[:n]
    x_buf, g_buf, s_buf, q_buf, k_buf, smoothed, q_sum, k_sum, squares_sum, sems, big_sems = rest[n:]
    rows, width = x_buf.shape
    queries = w_query.shape[1]
    steps = big_sems.shape[0] - 1
    depth = width // steps
    small = [
        pltpu.make_async_copy(source, target, sems.at[i])
        for i, (source, target) in enumerate([(residual, x_buf), (gain, g_buf), (smooth, s_buf)])
    ]
    for copy in small:
        copy.start()
    large = []
    for i in range(steps):
        part = pl.ds(i * depth, depth)
        large.append(pltpu.make_async_copy(w_query.at[part], q_buf.at[part], big_sems.at[i]))
    large.append(pltpu.make_async_copy(w_keyval, k_buf, big_sems.at[steps]))
    for copy in large:
        copy.start(priority=1)
    for copy in small:
        copy.wait()
    squares = jnp.zeros((rows, LANES), f32)
    for i in range(width // LANES):
        lanes = slice(i * LANES, (i + 1) * LANES)
        x = x_buf[:, lanes].astype(f32)
        squares += x * x
        smoothed[:, lanes] = (x * (g_buf[i : i + 1, :] / s_buf[i : i + 1, :])).astype(bf16)
    squares_sum[...] = jnp.broadcast_to(jnp.sum(squares, axis=1, keepdims=True), (rows, LANES))
    for i in range(steps):
        part = slice(i * depth, (i + 1) * depth)
        large[i].wait()
        term = jnp.dot(smoothed[:, part], q_buf[part, :], preferred_element_type=f32)
        if i == 0:
            q_sum[...] = term
        else:
            q_sum[...] += term
    large[steps].wait()
    k_sum[...] = jnp.dot(smoothed[...], k_buf[...], preferred_element_type=f32)
    me = lax.axis_index("gx")
    requests = rows // n
    columns = queries + k_buf.shape[1]
    for k in range(n):
        at = pl.ds(pl.multiple_of((me ^ k) * requests, requests), requests)
        outs[k][:, :queries] = q_sum[at, :]
        outs[k][:, queries:columns] = k_sum[at, :]
        outs[k][:, columns:] = squares_sum[at, :]


def project(n, residual, gain, smooth, w_query, w_keyval):
    rows, width = residual.shape
    columns = w_query.shape[1] + w_keyval.shape[1]
    steps = 8
    return pl.pallas_call(
        functools.partial(project_kernel, n),
        in_specs=[HBM] * 5,
        out_specs=[VMEM] * n,
        out_shape=[jax.ShapeDtypeStruct((rows // n, columns + LANES), f32)] * n,
        scratch_shapes=[
            pltpu.VMEM((rows, width), bf16),
            pltpu.VMEM((width // LANES, LANES), f32),
            pltpu.VMEM((width // LANES, LANES), f32),
            pltpu.VMEM(w_query.shape, bf16),
            pltpu.VMEM(w_keyval.shape, bf16),
            pltpu.VMEM((rows, width), bf16),
            pltpu.VMEM((rows, w_query.shape[1]), f32),
            pltpu.VMEM((rows, w_keyval.shape[1]), f32),
            pltpu.VMEM((rows, LANES), f32),
            pltpu.SemaphoreType.DMA((3,)),
            pltpu.SemaphoreType.DMA((steps + 1,)),
        ],
        compiler_params=params(60),
        name="project",
    )(residual, gain.reshape(-1, LANES), smooth.reshape(-1, LANES), w_query, w_keyval)


def norm_kernel(query_scale, keyval_scale, *refs):
    parts, out = refs[:-1], refs[-1]
    total = parts[0][...]
    for part in parts[1:]:
        total = total + part[...]
    columns = out.shape[1]
    row_scale = lax.rsqrt(total[:, columns : columns + 1] / D + EPSILON)
    tiles = query_scale.shape[0]
    for t in range(columns // LANES):
        scale = query_scale[t : t + 1, :] if t < tiles else keyval_scale[t - tiles : t - tiles + 1, :]
        lanes = slice(t * LANES, (t + 1) * LANES)
        out[:, lanes] = (row_scale * (total[:, lanes] * scale)).astype(bf16)


def norm(parts, query_scale, keyval_scale):
    rows, columns = parts[0].shape
    return pl.pallas_call(
        norm_kernel,
        in_specs=[VMEM] * (2 + len(parts)),
        out_specs=VMEM,
        out_shape=jax.ShapeDtypeStruct((rows, columns - LANES), bf16),
        compiler_params=params(8),
        name="norm",
    )(query_scale.reshape(-1, LANES), keyval_scale.reshape(-1, LANES), *parts)


def attend_kernel(n, *refs):
    pieces = refs[:n]
    lengths, keys, values, key_scale, value_scale, w_out = refs[n : n + 6]
    outs, w_head = refs[n + 6 : 2 * n + 6], refs[2 * n + 6]
    placed, k_buf, v_buf, q_rows, logits, messages, fresh, sems = refs[2 * n + 7 :]
    requests, _, local, _ = k_buf.shape
    load_keys = pltpu.make_async_copy(keys, k_buf, sems.at[0])
    load_values = pltpu.make_async_copy(values, v_buf, sems.at[1])
    load_weights = pltpu.make_async_copy(w_out.at[pl.ds(0, w_head.shape[0])], w_head, sems.at[2])
    load_keys.start()
    load_values.start()
    load_weights.start(priority=1)
    me = lax.axis_index("gx")
    for k in range(n):
        placed[me ^ k] = pieces[k][...].astype(f32)
    queries = HEADS * HEAD_DIM // n
    per = queries // LANES
    for h in range(HEADS):
        tile = placed[h // per, :, (h % per) * LANES : (h % per + 1) * LANES]
        q_rows[pl.ds(h, requests, stride=HEADS), :] = tile
    share = (placed.shape[2] - queries) // LANES
    for c in range(2 * KV_HEADS):
        start = queries + c % share * LANES
        fresh[pl.ds(c, requests, stride=2 * KV_HEADS), :] = placed[c // share, :, start : start + LANES]
    multiplier = HEAD_DIM ** (-0.5)
    load_keys.wait()
    for r in range(requests):
        for g in range(KV_HEADS):
            at = slice(r * HEADS + g * GROUP, r * HEADS + (g + 1) * GROUP)
            logits[at, :] = lax.dot_general(
                q_rows[at, :].astype(bf16), k_buf[r, g], (((1,), (1,)), ((), ())), preferred_element_type=f32
            )
    load_values.wait()
    position = lax.broadcasted_iota(jnp.int32, (GROUP, local), 1) + me * local
    first = me == 0
    count = requests * GROUP
    tops, totals = [[] for _ in range(n)], [[] for _ in range(n)]
    for r in range(requests):
        for g in range(KV_HEADS):
            row = r * HEADS + g * GROUP
            at = slice(row, row + GROUP)
            scale_at = r * KV_HEADS + g
            visible = position < lengths[r]
            scores = logits[at, :] * key_scale[scale_at : scale_at + 1, :] * multiplier
            scores = jnp.where(visible, scores, NEGATIVE)
            new_key = fresh[r * 2 * KV_HEADS + g : r * 2 * KV_HEADS + g + 1, :]
            new_value = fresh[r * 2 * KV_HEADS + KV_HEADS + g : r * 2 * KV_HEADS + KV_HEADS + g + 1, :]
            own = jnp.sum(q_rows[at, :] * new_key, axis=1, keepdims=True) * multiplier
            own = jnp.where(first, own, NEGATIVE)
            top = jnp.maximum(jnp.max(scores, axis=1, keepdims=True), own)
            weights = jnp.where(visible, jnp.exp(scores - top), 0.0)
            own_weight = jnp.where(first, jnp.exp(own - top), 0.0)
            totals[g].append(jnp.sum(weights, axis=1, keepdims=True) + own_weight)
            tops[g].append(top)
            scaled = (weights * value_scale[scale_at : scale_at + 1, :]).astype(bf16)
            mixed = jnp.dot(scaled, v_buf[r, g], preferred_element_type=f32) + own_weight * new_value
            messages[g, r * GROUP : (r + 1) * GROUP, :] = mixed
    diagonal = lax.broadcasted_iota(jnp.int32, (LANES, LANES), 0) == lax.broadcasted_iota(jnp.int32, (LANES, LANES), 1)
    wide = LANES // GROUP
    for p in range(n):
        rows = []
        for kind in (tops, totals):
            for b in range(count // LANES):
                column = jnp.concatenate(kind[p][b * wide : (b + 1) * wide], axis=0)
                rows.append(jnp.sum(jnp.where(diagonal, column, 0.0), axis=0, keepdims=True))
        spare = messages.shape[1] - count - len(rows)
        messages[p, count:, :] = jnp.concatenate(rows + [jnp.zeros((spare, LANES), f32)], axis=0)
    for k in range(n):
        outs[k][...] = messages[me ^ k]
    load_weights.wait()


def attend(n, pieces, lengths, keys, values, key_scale, value_scale, w_out):
    requests, _, local, _ = keys.shape
    count = requests * GROUP
    height = count + -(-2 * count // LANES // 8) * 8
    return pl.pallas_call(
        functools.partial(attend_kernel, n),
        in_specs=[VMEM] * n + [SMEM, HBM, HBM, VMEM, VMEM, HBM],
        out_specs=[VMEM] * (n + 1),
        out_shape=[jax.ShapeDtypeStruct((height, LANES), f32)] * n
        + [jax.ShapeDtypeStruct((w_out.shape[0] // 2, w_out.shape[1]), bf16)],
        scratch_shapes=[
            pltpu.VMEM((n,) + pieces[0].shape, f32),
            pltpu.VMEM(keys.shape, bf16),
            pltpu.VMEM(values.shape, bf16),
            pltpu.VMEM((requests * HEADS, HEAD_DIM), f32),
            pltpu.VMEM((requests * HEADS, local), f32),
            pltpu.VMEM((n, height, LANES), f32),
            pltpu.VMEM((requests * 2 * KV_HEADS, HEAD_DIM), f32),
            pltpu.SemaphoreType.DMA((3,)),
        ],
        compiler_params=params(30),
        name="attend",
    )(*pieces, lengths, keys, values, key_scale.reshape(-1, local), value_scale.reshape(-1, local), w_out)


def merge_kernel(*refs):
    parts, out, mixed = refs[:-2], refs[-2], refs[-1]
    count = mixed.shape[0]
    requests = out.shape[0]
    diagonal = lax.broadcasted_iota(jnp.int32, (LANES, LANES), 0) == lax.broadcasted_iota(jnp.int32, (LANES, LANES), 1)
    blocks = count // LANES
    for b in range(blocks):
        at = slice(b * LANES, (b + 1) * LANES)
        tops = [part[count + b : count + b + 1, :] for part in parts]
        totals = [part[count + blocks + b : count + blocks + b + 1, :] for part in parts]
        largest = tops[0]
        for top in tops[1:]:
            largest = jnp.maximum(largest, top)
        factors = [jnp.exp(top - largest) for top in tops]
        total = factors[0] * totals[0]
        for factor, other in zip(factors[1:], totals[1:]):
            total = total + factor * other
        sums = None
        for factor, part in zip(factors, parts):
            column = jnp.sum(jnp.where(diagonal, factor, 0.0), axis=1, keepdims=True)
            term = column * part[at, :]
            sums = term if sums is None else sums + term
        column = jnp.sum(jnp.where(diagonal, total, 0.0), axis=1, keepdims=True)
        mixed[at, :] = sums / column
    for h in range(count // requests):
        out[:, h * HEAD_DIM : (h + 1) * HEAD_DIM] = mixed[pl.ds(h, requests, stride=count // requests), :].astype(bf16)


def merge(parts, requests):
    count = requests * GROUP
    return pl.pallas_call(
        merge_kernel,
        in_specs=[VMEM] * len(parts),
        out_specs=VMEM,
        out_shape=jax.ShapeDtypeStruct((requests, GROUP * HEAD_DIM), bf16),
        scratch_shapes=[pltpu.VMEM((count, HEAD_DIM), f32)],
        compiler_params=params(8),
        name="merge",
    )(*parts)


def output_kernel(n, *refs):
    pieces = refs[:n]
    w_head, w_out, out_scale, ffn, kept, given, w_buf, ffn_buf, total, placed, sems = refs[n:]
    rest, width = w_buf.shape
    steps = sems.shape[0] - 1
    depth, head = rest // steps, w_head.shape[0]
    copies = []
    for i in range(steps):
        part = pl.ds(i * depth, depth)
        source = w_out.at[pl.ds(head + i * depth, depth)]
        copies.append(pltpu.make_async_copy(source, w_buf.at[part], sems.at[i]))
        copies[-1].start(priority=1)
    load = pltpu.make_async_copy(ffn, ffn_buf, sems.at[steps])
    load.start()
    me = lax.axis_index("gx")
    for k in range(n):
        placed[me ^ k] = pieces[k][...].astype(f32)
    attended = placed[...].reshape(total.shape[0], head + rest).astype(bf16)
    total[...] = jnp.dot(attended[:, :head], w_head[...], preferred_element_type=f32)
    for i in range(steps):
        part = slice(i * depth, (i + 1) * depth)
        copies[i].wait()
        total[...] += jnp.dot(attended[:, head:][:, part], w_buf[part, :], preferred_element_type=f32)
    load.wait()
    for t in range(width // LANES):
        lanes = slice(t * LANES, (t + 1) * LANES)
        total[:, lanes] = total[:, lanes] * out_scale[t : t + 1, :] + ffn_buf[:, lanes]
    rows = total.shape[0] // 2
    core = lax.axis_index("gy") & 1
    kept[...] = total[pl.ds(pl.multiple_of(core * rows, rows), rows), :]
    given[...] = total[pl.ds(pl.multiple_of((1 - core) * rows, rows), rows), :]


def output(pieces, w_head, w_out, out_scale, ffn):
    n = len(pieces)
    rows = ffn.shape[0]
    width = w_out.shape[1]
    steps = 4
    return pl.pallas_call(
        functools.partial(output_kernel, n),
        in_specs=[VMEM] * (n + 1) + [HBM, VMEM, HBM],
        out_specs=[VMEM] * 2,
        out_shape=[jax.ShapeDtypeStruct((rows // 2, width), f32)] * 2,
        scratch_shapes=[
            pltpu.VMEM((w_out.shape[0] - w_head.shape[0], width), bf16),
            pltpu.VMEM((rows, width), f32),
            pltpu.VMEM((rows, width), f32),
            pltpu.VMEM((n,) + pieces[0].shape, f32),
            pltpu.SemaphoreType.DMA((steps + 1,)),
        ],
        compiler_params=params(30),
        name="output",
    )(*pieces, w_head, w_out, out_scale.reshape(-1, LANES), ffn)


def body(n_gx, n_gy, residual, ffn_partial, norm_gain, smooth_scale, w_query, query_scale, w_keyval, keyval_scale,
         key_cache, value_cache, key_scale, value_scale, lengths, w_out, out_scale):
    gy = lax.axis_index("gy")
    rows = residual.shape[0]
    requests = rows // n_gy
    parts = project(n_gx, residual, norm_gain, smooth_scale, w_query, w_keyval)
    pieces = spread(norm(trade(parts, "gx", n_gx), query_scale, keyval_scale), n_gx)
    *parts, w_head = attend(n_gx, pieces, lengths, key_cache, value_cache, key_scale, value_scale, w_out)
    pieces = spread(merge(trade(parts, "gx", n_gx), requests), n_gx)
    kept, given = output(pieces, w_head, w_out, out_scale, ffn_partial[0])
    core = gy & 1
    chip = kept + swap(given, "gy", n_gy, 1)
    whole = chip + swap(chip, "gy", n_gy, 2)
    mine = lax.dynamic_slice_in_dim(residual, core * (rows // 2), rows // 2, 0)
    mine = (mine.astype(f32) + whole).astype(bf16)
    return jnp.concatenate(ordered([mine, swap(mine, "gy", n_gy, 1)], core))


def joined(value, axis, join):
    pieces = jax.tree.map(lambda part: lax.all_gather(part, axis), value)
    head = jax.tree.map(lambda part: part[0], pieces)
    tail = jax.tree.map(lambda part: part[1:], pieces)
    subtotal, _ = lax.scan(lambda subtotal, piece: (join(subtotal, piece), None), head, tail)
    return subtotal


def combine(former, latter):
    top = jnp.maximum(former[0], latter[0])
    first_factor = jnp.exp(former[0] - top)
    second_factor = jnp.exp(latter[0] - top)
    total = former[1] * first_factor + latter[1] * second_factor
    mixed = former[2] * first_factor[..., None] + latter[2] * second_factor[..., None]
    return (top, total, mixed)


def plain_body(
    residual,
    ffn_partial,
    norm_gain,
    smooth_scale,
    w_query,
    query_scale,
    w_keyval,
    keyval_scale,
    key_cache,
    value_cache,
    key_scale,
    value_scale,
    lengths,
    w_out,
    out_scale,
):
    widened = residual.astype(jnp.float32)
    ffn_total = lax.psum(ffn_partial[0], "gy")
    squares = jnp.sum(widened * widened, axis=1)
    smoothed = (widened * (norm_gain / smooth_scale)).astype(jnp.bfloat16)
    query_part = jnp.dot(smoothed, w_query, preferred_element_type=jnp.float32) * query_scale
    keyval_part = jnp.dot(smoothed, w_keyval, preferred_element_type=jnp.float32) * keyval_scale
    query_sum, keyval_sum, square_sum = lax.psum((query_part, keyval_part, squares), "gx")
    row_scale = lax.rsqrt(square_sum / D + EPSILON)[:, None]
    query_rows = (row_scale * query_sum).astype(jnp.bfloat16)
    keyval_rows = (row_scale * keyval_sum).astype(jnp.bfloat16)
    query_vectors, keyvals = (
        lax.all_to_all(query_rows, "gy", split_axis=0, concat_axis=1, tiled=True),
        lax.all_to_all(keyval_rows, "gy", split_axis=0, concat_axis=1, tiled=True),
    )
    requests = query_vectors.shape[0]
    local = key_cache.shape[2]
    group = HEADS // KV_HEADS
    score_multiplier = HEAD_DIM ** (-0.5)
    grouped = query_vectors.reshape(requests, KV_HEADS, group, HEAD_DIM)
    fresh_key_rows = keyvals[:, : KV_HEADS * HEAD_DIM].reshape(requests, KV_HEADS, HEAD_DIM)
    fresh_value_rows = keyvals[:, KV_HEADS * HEAD_DIM :].reshape(requests, KV_HEADS, HEAD_DIM)
    logit_scores = jnp.einsum(
        "rgqd,rgsd->rgqs", grouped, key_cache, preferred_element_type=jnp.float32
    )
    logit_scores = logit_scores * key_scale[:, :, None, :] * score_multiplier
    position = lax.axis_index("gx") * local + jnp.arange(local, dtype=jnp.int32)
    visible = (position[None, :] < lengths[:, None])[:, None, None, :]
    logit_scores = jnp.where(visible, logit_scores, NEGATIVE)
    local_top = jnp.max(logit_scores, axis=-1)
    weights = jnp.where(visible, jnp.exp(logit_scores - local_top[..., None]), 0.0)
    local_total = jnp.sum(weights, axis=-1)
    scaled = (weights * value_scale[:, :, None, :]).astype(jnp.bfloat16)
    local_mixed = jnp.einsum(
        "rgqs,rgsd->rgqd", scaled, value_cache, preferred_element_type=jnp.float32
    )
    top, total, mixed = joined((local_top, local_total, local_mixed), "gx", combine)
    own = (
        jnp.einsum("rgqd,rgd->rgq", grouped, fresh_key_rows, preferred_element_type=jnp.float32)
        * score_multiplier
    )
    largest = jnp.maximum(top, own)
    old_factor = jnp.exp(top - largest)
    own_weight = jnp.exp(own - largest)
    total = total * old_factor + own_weight
    mixed = (
        mixed * old_factor[..., None]
        + own_weight[..., None] * fresh_value_rows.astype(jnp.float32)[:, :, None, :]
    )
    attended = (mixed / total[..., None]).astype(jnp.bfloat16).reshape(requests, HEADS * HEAD_DIM)
    head_block = lax.all_to_all(attended, "gy", split_axis=1, concat_axis=0, tiled=True)
    projected = jnp.dot(head_block, w_out, preferred_element_type=jnp.float32) * out_scale
    attention_total = lax.psum(projected, "gy")
    new_residual = (widened + ffn_total + attention_total).astype(jnp.bfloat16)
    return new_residual


def solution(mesh):
    placed = (
        P("rep", "gx"), P("gy", "rep", "gx"), P("gx"), P("gx"), P("gx", "gy"), P("gy"), P("gx", "gy"), P("gy"),
        P(("rep", "gy"), None, "gx", None), P(("rep", "gy"), None, "gx", None),
        P(("rep", "gy"), None, "gx"), P(("rep", "gy"), None, "gx"), P(("rep", "gy")), P("gy", "gx"), P("gx"),
    )
    n_gx, n_gy = mesh.shape["gx"], mesh.shape["gy"]

    def run(*arrays):
        if n_gx == 4 and n_gy == 4:
            return body(n_gx, n_gy, *arrays)
        return plain_body(*arrays)

    return jax.shard_map(run, mesh=mesh, in_specs=placed, out_specs=P("rep", "gx"), check_vma=False)
```

```python
import functools

import jax
import jax.numpy as jnp
from jax import lax
from jax.experimental import pallas as pl
from jax.experimental.pallas import tpu as pltpu
from jax.sharding import PartitionSpec as P

D = 16384
HEADS = 64
KV_HEADS = 4
HEAD_DIM = 128
GROUP = HEADS // KV_HEADS
EPSILON = 1e-05
NEGATIVE = -1e30
LANES = 128
SHRINK = 32.0
f32 = jnp.float32
bf16 = jnp.bfloat16
VMEM = pl.BlockSpec(memory_space=pltpu.VMEM)
SMEM = pl.BlockSpec(memory_space=pltpu.SMEM)
ANY = pl.BlockSpec(memory_space=pl.ANY)
HBM = pl.BlockSpec(memory_space=pltpu.HBM)


def partners(n, offset):
    return [(i, i ^ offset) for i in range(n)]


def ordered(pieces, me):
    n = len(pieces)
    return [lax.select_n(me, *[pieces[j ^ i] for i in range(n)]) for j in range(n)]


def trade(chunks, axis, n):
    return [chunks[0]] + [lax.ppermute(chunks[k], axis, partners(n, k)) for k in range(1, n)]


def place(placed, pieces, n):
    me = lax.axis_index("gx")
    for k in range(n):
        placed[me ^ k] = pieces[k][...].astype(f32)

    @pl.when(me == lax.axis_index("gy"))
    def _():
        placed[me] = pieces[n][...].astype(f32)


def spread(value, n):
    pieces = []
    for k in range(n):
        pairs = [(a * n + b, (b ^ k) * n + a) for a in range(n) for b in range(n)]
        pieces.append(lax.ppermute(value, ("gx", "gy"), [pair for pair in pairs if pair[0] != pair[1]]))
    return pieces + [value]


def swap(value, axis, n, offset):
    return lax.ppermute(value, axis, partners(n, offset))


def params(mib):
    return pltpu.CompilerParams(vmem_limit_bytes=mib << 20)


def project_kernel(n, residual, gain, smooth, w_query, w_keyval, *rest):
    outs = rest[:n]
    x_buf, g_buf, s_buf, q_buf, k_buf, smoothed, q_sum, k_sum, squares_sum, sems, big_sems = rest[n:]
    rows, width = x_buf.shape
    queries = w_query.shape[1]
    steps = big_sems.shape[0] - 1
    depth = width // steps
    small = [
        pltpu.make_async_copy(source, target, sems.at[i])
        for i, (source, target) in enumerate([(residual, x_buf), (gain, g_buf), (smooth, s_buf)])
    ]
    for copy in small:
        copy.start()
    large = []
    for i in range(steps):
        part = pl.ds(i * depth, depth)
        large.append(pltpu.make_async_copy(w_query.at[part], q_buf.at[part], big_sems.at[i]))
    large.append(pltpu.make_async_copy(w_keyval, k_buf, big_sems.at[steps]))
    for copy in large:
        copy.start(priority=1)
    for copy in small:
        copy.wait()
    squares = jnp.zeros((rows, LANES), f32)
    for i in range(width // LANES):
        lanes = slice(i * LANES, (i + 1) * LANES)
        x = x_buf[:, lanes].astype(f32)
        squares += x * x
        smoothed[:, lanes] = (x * (g_buf[i : i + 1, :] / s_buf[i : i + 1, :])).astype(bf16)
    squares_sum[...] = jnp.broadcast_to(jnp.sum(squares, axis=1, keepdims=True), (rows, LANES))
    for i in range(steps):
        part = slice(i * depth, (i + 1) * depth)
        large[i].wait()
        term = jnp.dot(smoothed[:, part], q_buf[part, :], preferred_element_type=f32)
        if i == 0:
            q_sum[...] = term
        else:
            q_sum[...] += term
    large[steps].wait()
    k_sum[...] = jnp.dot(smoothed[...], k_buf[...], preferred_element_type=f32)
    me = lax.axis_index("gx")
    requests = rows // n
    columns = queries + k_buf.shape[1]
    for k in range(n):
        at = pl.ds(pl.multiple_of((me ^ k) * requests, requests), requests)
        outs[k][:, :queries] = q_sum[at, :]
        outs[k][:, queries:columns] = k_sum[at, :]
        outs[k][:, columns:] = squares_sum[at, :]


def project(n, residual, gain, smooth, w_query, w_keyval):
    rows, width = residual.shape
    columns = w_query.shape[1] + w_keyval.shape[1]
    steps = 8
    return pl.pallas_call(
        functools.partial(project_kernel, n),
        in_specs=[HBM] * 5,
        out_specs=[VMEM] * n,
        out_shape=[jax.ShapeDtypeStruct((rows // n, columns + LANES), f32)] * n,
        scratch_shapes=[
            pltpu.VMEM((rows, width), bf16),
            pltpu.VMEM((width // LANES, LANES), f32),
            pltpu.VMEM((width // LANES, LANES), f32),
            pltpu.VMEM(w_query.shape, bf16),
            pltpu.VMEM(w_keyval.shape, bf16),
            pltpu.VMEM((rows, width), bf16),
            pltpu.VMEM((rows, w_query.shape[1]), f32),
            pltpu.VMEM((rows, w_keyval.shape[1]), f32),
            pltpu.VMEM((rows, LANES), f32),
            pltpu.SemaphoreType.DMA((3,)),
            pltpu.SemaphoreType.DMA((steps + 1,)),
        ],
        compiler_params=params(60),
        name="project",
    )(residual, gain.reshape(-1, LANES), smooth.reshape(-1, LANES), w_query, w_keyval)


def norm_kernel(query_scale, keyval_scale, *refs):
    parts, out = refs[:-1], refs[-1]
    total = parts[0][...]
    for part in parts[1:]:
        total = total + part[...]
    columns = out.shape[1]
    row_scale = lax.rsqrt(total[:, columns : columns + 1] / D + EPSILON)
    tiles = query_scale.shape[0]
    for t in range(columns // LANES):
        scale = query_scale[t : t + 1, :] if t < tiles else keyval_scale[t - tiles : t - tiles + 1, :]
        lanes = slice(t * LANES, (t + 1) * LANES)
        out[:, lanes] = (row_scale * (total[:, lanes] * scale)).astype(bf16)


def norm(parts, query_scale, keyval_scale):
    rows, columns = parts[0].shape
    return pl.pallas_call(
        norm_kernel,
        in_specs=[VMEM] * (2 + len(parts)),
        out_specs=VMEM,
        out_shape=jax.ShapeDtypeStruct((rows, columns - LANES), bf16),
        compiler_params=params(8),
        name="norm",
    )(query_scale.reshape(-1, LANES), keyval_scale.reshape(-1, LANES), *parts)


def fetch_kernel(n, *refs):
    sources, targets, sems = refs[1 : n + 1], refs[n + 1 : 2 * n + 1], refs[-1]
    copies = [pltpu.make_async_copy(a, b, sems.at[i]) for i, (a, b) in enumerate(zip(sources, targets))]
    for copy in copies:
        copy.start()
    for copy in copies:
        copy.wait()


def fetch(after, *arrays):
    n = len(arrays)
    size = sum(array.size * array.dtype.itemsize for array in arrays)
    return pl.pallas_call(
        functools.partial(fetch_kernel, n),
        in_specs=[ANY] + [HBM] * n,
        out_specs=[VMEM] * n,
        out_shape=[jax.ShapeDtypeStruct(array.shape, array.dtype) for array in arrays],
        scratch_shapes=[pltpu.SemaphoreType.DMA((n,))],
        compiler_params=params(24),
        cost_estimate=pl.CostEstimate(flops=0, bytes_accessed=2 * size, transcendentals=0),
        name="fetch",
    )(after, *arrays)


def attend_kernel(n, *refs):
    pieces, refs = refs[: n + 1], refs[n + 1 :]
    lengths, keys, values, key_scale, value_scale = refs[:5]
    outs = refs[5 : n + 5]
    placed, q_rows, logits, messages, fresh = refs[n + 5 :]
    requests, _, local, _ = keys.shape
    me = lax.axis_index("gx")
    place(placed, pieces, n)
    queries = HEADS * HEAD_DIM // n
    per = queries // LANES
    for h in range(HEADS):
        tile = placed[h // per, :, (h % per) * LANES : (h % per + 1) * LANES]
        q_rows[pl.ds(h, requests, stride=HEADS), :] = tile
    share = (placed.shape[2] - queries) // LANES
    for c in range(2 * KV_HEADS):
        start = queries + c % share * LANES
        fresh[pl.ds(c, requests, stride=2 * KV_HEADS), :] = placed[c // share, :, start : start + LANES]
    multiplier = HEAD_DIM ** (-0.5)
    for r in range(requests):
        for g in range(KV_HEADS):
            at = slice(r * HEADS + g * GROUP, r * HEADS + (g + 1) * GROUP)
            logits[at, :] = lax.dot_general(
                q_rows[at, :].astype(bf16), keys[r, g], (((1,), (1,)), ((), ())), preferred_element_type=f32
            )
    position = lax.broadcasted_iota(jnp.int32, (GROUP, local), 1) + me * local
    first = me == 0
    count = requests * GROUP
    tops, totals = [[] for _ in range(n)], [[] for _ in range(n)]
    for r in range(requests):
        for g in range(KV_HEADS):
            row = r * HEADS + g * GROUP
            at = slice(row, row + GROUP)
            scale_at = r * KV_HEADS + g
            visible = position < lengths[r]
            scores = logits[at, :] * key_scale[scale_at : scale_at + 1, :] * multiplier
            scores = jnp.where(visible, scores, NEGATIVE)
            new_key = fresh[r * 2 * KV_HEADS + g : r * 2 * KV_HEADS + g + 1, :]
            new_value = fresh[r * 2 * KV_HEADS + KV_HEADS + g : r * 2 * KV_HEADS + KV_HEADS + g + 1, :]
            own = jnp.sum(q_rows[at, :] * new_key, axis=1, keepdims=True) * multiplier
            own = jnp.where(first, own, NEGATIVE)
            top = jnp.maximum(jnp.max(scores, axis=1, keepdims=True), own)
            weights = jnp.where(visible, jnp.exp(scores - top), 0.0)
            own_weight = jnp.where(first, jnp.exp(own - top), 0.0)
            totals[g].append(jnp.sum(weights, axis=1, keepdims=True) + own_weight)
            tops[g].append(top)
            scaled = (weights * value_scale[scale_at : scale_at + 1, :]).astype(bf16)
            mixed = jnp.dot(scaled, values[r, g], preferred_element_type=f32) + own_weight * new_value
            messages[g, r * GROUP : (r + 1) * GROUP, :] = mixed
    diagonal = lax.broadcasted_iota(jnp.int32, (LANES, LANES), 0) == lax.broadcasted_iota(jnp.int32, (LANES, LANES), 1)
    wide = LANES // GROUP
    for p in range(n):
        rows = []
        for kind in (tops, totals):
            for b in range(count // LANES):
                column = jnp.concatenate(kind[p][b * wide : (b + 1) * wide], axis=0)
                rows.append(jnp.sum(jnp.where(diagonal, column, 0.0), axis=0, keepdims=True))
        spare = messages.shape[1] - count - len(rows)
        messages[p, count:, :] = jnp.concatenate(rows + [jnp.zeros((spare, LANES), f32)], axis=0)
    for k in range(n):
        outs[k][...] = messages[me ^ k]


def attend(n, pieces, lengths, keys, values, key_scale, value_scale):
    requests, _, local, _ = keys.shape
    count = requests * GROUP
    height = count + -(-2 * count // LANES // 8) * 8
    return pl.pallas_call(
        functools.partial(attend_kernel, n),
        in_specs=[VMEM] * (n + 1) + [SMEM, VMEM, VMEM, VMEM, VMEM],
        out_specs=[VMEM] * n,
        out_shape=[jax.ShapeDtypeStruct((height, LANES), f32)] * n,
        scratch_shapes=[
            pltpu.VMEM((n,) + pieces[0].shape, f32),
            pltpu.VMEM((requests * HEADS, HEAD_DIM), f32),
            pltpu.VMEM((requests * HEADS, local), f32),
            pltpu.VMEM((n, height, LANES), f32),
            pltpu.VMEM((requests * 2 * KV_HEADS, HEAD_DIM), f32),
        ],
        compiler_params=params(24),
        name="attend",
    )(*pieces, lengths, keys, values, key_scale.reshape(-1, local), value_scale.reshape(-1, local))


def merge_kernel(*refs):
    parts, out, mixed = refs[:-2], refs[-2], refs[-1]
    count = mixed.shape[0]
    requests = out.shape[0]
    diagonal = lax.broadcasted_iota(jnp.int32, (LANES, LANES), 0) == lax.broadcasted_iota(jnp.int32, (LANES, LANES), 1)
    blocks = count // LANES
    for b in range(blocks):
        at = slice(b * LANES, (b + 1) * LANES)
        tops = [part[count + b : count + b + 1, :] for part in parts]
        totals = [part[count + blocks + b : count + blocks + b + 1, :] for part in parts]
        largest = tops[0]
        for top in tops[1:]:
            largest = jnp.maximum(largest, top)
        factors = [jnp.exp(top - largest) for top in tops]
        total = factors[0] * totals[0]
        for factor, other in zip(factors[1:], totals[1:]):
            total = total + factor * other
        sums = None
        for factor, part in zip(factors, parts):
            column = jnp.sum(jnp.where(diagonal, factor, 0.0), axis=1, keepdims=True)
            term = column * part[at, :]
            sums = term if sums is None else sums + term
        column = jnp.sum(jnp.where(diagonal, total, 0.0), axis=1, keepdims=True)
        mixed[at, :] = sums / column
    for h in range(count // requests):
        out[:, h * HEAD_DIM : (h + 1) * HEAD_DIM] = mixed[pl.ds(h, requests, stride=count // requests), :].astype(bf16)


def merge(parts, requests):
    count = requests * GROUP
    return pl.pallas_call(
        merge_kernel,
        in_specs=[VMEM] * len(parts),
        out_specs=VMEM,
        out_shape=jax.ShapeDtypeStruct((requests, GROUP * HEAD_DIM), bf16),
        scratch_shapes=[pltpu.VMEM((count, HEAD_DIM), f32)],
        compiler_params=params(8),
        name="merge",
    )(*parts)


def output_kernel(n, *refs):
    pieces = refs[: n + 1]
    w_out, out_scale, ffn, kept, given, total, placed = refs[n + 1 :]
    width = w_out.shape[1]
    place(placed, pieces, n)
    attended = placed[...].reshape(total.shape[0], w_out.shape[0]).astype(bf16)
    span = width // 4
    for i in range(4):
        part = slice(i * span, (i + 1) * span)
        total[:, part] = jnp.dot(attended, w_out[:, part], preferred_element_type=f32)
    for t in range(width // LANES):
        lanes = slice(t * LANES, (t + 1) * LANES)
        total[:, lanes] = total[:, lanes] * out_scale[t : t + 1, :] + ffn[:, lanes]
    rows = total.shape[0] // 2
    core = lax.axis_index("gy") & 1
    kept[...] = total[pl.ds(pl.multiple_of(core * rows, rows), rows), :]
    given[...] = total[pl.ds(pl.multiple_of((1 - core) * rows, rows), rows), :]


def output(pieces, w_out, out_scale, ffn):
    n = len(pieces) - 1
    rows, width = ffn.shape
    return pl.pallas_call(
        functools.partial(output_kernel, n),
        in_specs=[VMEM] * (n + 4),
        out_specs=[VMEM] * 2,
        out_shape=[jax.ShapeDtypeStruct((rows // 2, width), f32)] * 2,
        scratch_shapes=[pltpu.VMEM((rows, width), f32), pltpu.VMEM((n,) + pieces[0].shape, f32)],
        compiler_params=params(20),
        name="output",
    )(*pieces, w_out, out_scale.reshape(-1, LANES), ffn)


def body(n_gx, n_gy, residual, ffn_partial, norm_gain, smooth_scale, w_query, query_scale, w_keyval, keyval_scale,
         key_cache, value_cache, key_scale, value_scale, lengths, w_out, out_scale):
    gy = lax.axis_index("gy")
    rows = residual.shape[0]
    requests = rows // n_gy
    parts = project(n_gx, residual, norm_gain, smooth_scale, w_query, w_keyval)
    (w_near,) = fetch(parts[0], w_out)
    total = trade(parts, "gx", n_gx)
    total[0], w_near = lax.optimization_barrier((total[0], w_near))
    pieces = spread(norm(total, query_scale, keyval_scale), n_gx)
    parts = attend(n_gx, pieces, lengths, key_cache, value_cache, key_scale, value_scale)
    pieces = spread(merge(trade(parts, "gx", n_gx), requests), n_gx)
    kept, given = output(pieces, w_near, out_scale, ffn_partial[0])
    core = gy & 1
    chip = kept + swap(given, "gy", n_gy, 1)
    other = swap((chip * (1 / SHRINK)).astype(jnp.float16), "gy", n_gy, 2)
    whole = chip + other.astype(f32) * SHRINK
    mine = lax.dynamic_slice_in_dim(residual, core * (rows // 2), rows // 2, 0)
    mine = (mine.astype(f32) + whole).astype(bf16)
    return jnp.concatenate(ordered([mine, swap(mine, "gy", n_gy, 1)], core))


def joined(value, axis, join):
    pieces = jax.tree.map(lambda part: lax.all_gather(part, axis), value)
    head = jax.tree.map(lambda part: part[0], pieces)
    tail = jax.tree.map(lambda part: part[1:], pieces)
    subtotal, _ = lax.scan(lambda subtotal, piece: (join(subtotal, piece), None), head, tail)
    return subtotal


def combine(former, latter):
    top = jnp.maximum(former[0], latter[0])
    first_factor = jnp.exp(former[0] - top)
    second_factor = jnp.exp(latter[0] - top)
    total = former[1] * first_factor + latter[1] * second_factor
    mixed = former[2] * first_factor[..., None] + latter[2] * second_factor[..., None]
    return (top, total, mixed)


def plain_body(
    residual,
    ffn_partial,
    norm_gain,
    smooth_scale,
    w_query,
    query_scale,
    w_keyval,
    keyval_scale,
    key_cache,
    value_cache,
    key_scale,
    value_scale,
    lengths,
    w_out,
    out_scale,
):
    widened = residual.astype(jnp.float32)
    ffn_total = lax.psum(ffn_partial[0], "gy")
    squares = jnp.sum(widened * widened, axis=1)
    smoothed = (widened * (norm_gain / smooth_scale)).astype(jnp.bfloat16)
    query_part = jnp.dot(smoothed, w_query, preferred_element_type=jnp.float32) * query_scale
    keyval_part = jnp.dot(smoothed, w_keyval, preferred_element_type=jnp.float32) * keyval_scale
    query_sum, keyval_sum, square_sum = lax.psum((query_part, keyval_part, squares), "gx")
    row_scale = lax.rsqrt(square_sum / D + EPSILON)[:, None]
    query_rows = (row_scale * query_sum).astype(jnp.bfloat16)
    keyval_rows = (row_scale * keyval_sum).astype(jnp.bfloat16)
    query_vectors, keyvals = (
        lax.all_to_all(query_rows, "gy", split_axis=0, concat_axis=1, tiled=True),
        lax.all_to_all(keyval_rows, "gy", split_axis=0, concat_axis=1, tiled=True),
    )
    requests = query_vectors.shape[0]
    local = key_cache.shape[2]
    group = HEADS // KV_HEADS
    score_multiplier = HEAD_DIM ** (-0.5)
    grouped = query_vectors.reshape(requests, KV_HEADS, group, HEAD_DIM)
    fresh_key_rows = keyvals[:, : KV_HEADS * HEAD_DIM].reshape(requests, KV_HEADS, HEAD_DIM)
    fresh_value_rows = keyvals[:, KV_HEADS * HEAD_DIM :].reshape(requests, KV_HEADS, HEAD_DIM)
    logit_scores = jnp.einsum(
        "rgqd,rgsd->rgqs", grouped, key_cache, preferred_element_type=jnp.float32
    )
    logit_scores = logit_scores * key_scale[:, :, None, :] * score_multiplier
    position = lax.axis_index("gx") * local + jnp.arange(local, dtype=jnp.int32)
    visible = (position[None, :] < lengths[:, None])[:, None, None, :]
    logit_scores = jnp.where(visible, logit_scores, NEGATIVE)
    local_top = jnp.max(logit_scores, axis=-1)
    weights = jnp.where(visible, jnp.exp(logit_scores - local_top[..., None]), 0.0)
    local_total = jnp.sum(weights, axis=-1)
    scaled = (weights * value_scale[:, :, None, :]).astype(jnp.bfloat16)
    local_mixed = jnp.einsum(
        "rgqs,rgsd->rgqd", scaled, value_cache, preferred_element_type=jnp.float32
    )
    top, total, mixed = joined((local_top, local_total, local_mixed), "gx", combine)
    own = (
        jnp.einsum("rgqd,rgd->rgq", grouped, fresh_key_rows, preferred_element_type=jnp.float32)
        * score_multiplier
    )
    largest = jnp.maximum(top, own)
    old_factor = jnp.exp(top - largest)
    own_weight = jnp.exp(own - largest)
    total = total * old_factor + own_weight
    mixed = (
        mixed * old_factor[..., None]
        + own_weight[..., None] * fresh_value_rows.astype(jnp.float32)[:, :, None, :]
    )
    attended = (mixed / total[..., None]).astype(jnp.bfloat16).reshape(requests, HEADS * HEAD_DIM)
    head_block = lax.all_to_all(attended, "gy", split_axis=1, concat_axis=0, tiled=True)
    projected = jnp.dot(head_block, w_out, preferred_element_type=jnp.float32) * out_scale
    attention_total = lax.psum(projected, "gy")
    new_residual = (widened + ffn_total + attention_total).astype(jnp.bfloat16)
    return new_residual


def solution(mesh):
    placed = (
        P("rep", "gx"), P("gy", "rep", "gx"), P("gx"), P("gx"), P("gx", "gy"), P("gy"), P("gx", "gy"), P("gy"),
        P(("rep", "gy"), None, "gx", None), P(("rep", "gy"), None, "gx", None),
        P(("rep", "gy"), None, "gx"), P(("rep", "gy"), None, "gx"), P(("rep", "gy")), P("gy", "gx"), P("gx"),
    )
    n_gx, n_gy = mesh.shape["gx"], mesh.shape["gy"]

    def run(*arrays):
        if n_gx == 4 and n_gy == 4:
            return body(n_gx, n_gy, *arrays)
        return plain_body(*arrays)

    return jax.shard_map(run, mesh=mesh, in_specs=placed, out_specs=P("rep", "gx"), check_vma=False)
```

```python
import functools

import jax
import jax.numpy as jnp
from jax import lax
from jax.experimental import pallas as pl
from jax.experimental.pallas import tpu as pltpu
from jax.sharding import PartitionSpec as P

D = 16384
HEADS = 64
KV_HEADS = 4
HEAD_DIM = 128
GROUP = HEADS // KV_HEADS
EPSILON = 1e-05
NEGATIVE = -1e30
LANES = 128
LOWEST = -4e7
UNITS = (32768.0, 16.0, 0.0078125)
SHRINK = 32.0
f32 = jnp.float32
bf16 = jnp.bfloat16
VMEM = pl.BlockSpec(memory_space=pltpu.VMEM)
SMEM = pl.BlockSpec(memory_space=pltpu.SMEM)
ANY = pl.BlockSpec(memory_space=pl.ANY)
HBM = pl.BlockSpec(memory_space=pltpu.HBM)


def partners(n, offset):
    return [(i, i ^ offset) for i in range(n)]


def ordered(pieces, me):
    n = len(pieces)
    return [lax.select_n(me, *[pieces[j ^ i] for i in range(n)]) for j in range(n)]


def trade(chunks, axis, n):
    return [chunks[0]] + [lax.ppermute(chunks[k], axis, partners(n, k)) for k in (3, 1, 2)]


def place(placed, pieces, n):
    gx = lax.axis_index("gx")
    for k in range(n // 2):
        for core in range(2):
            placed[2 * ((gx // 2) ^ k) + core] = pieces[k][core].astype(f32)

    @pl.when(gx == lax.axis_index("gy"))
    def _():
        for core in range(2):
            placed[2 * (gx // 2) + core] = pieces[n // 2][core].astype(f32)


def pair_kernel(mine, other, out):
    core = lax.axis_index("gy") & 1
    out[core] = mine[...]
    out[1 - core] = other[...]


def spread(value, n):
    pair = pl.pallas_call(
        pair_kernel,
        in_specs=[VMEM] * 2,
        out_specs=VMEM,
        out_shape=jax.ShapeDtypeStruct((2,) + value.shape, value.dtype),
        compiler_params=params(4),
        name="pair",
    )(value, swap(value, "gy", n, 1))
    pieces = []
    for k in range(n // 2):
        pairs = [(a * n + b, (b % 2 + 2 * ((b // 2) ^ k)) * n + a) for a in range(n) for b in range(n)]
        pieces.append(lax.ppermute(pair, ("gx", "gy"), [p for p in pairs if p[0] != p[1]]))
    return pieces + [pair]


def swap(value, axis, n, offset):
    return lax.ppermute(value, axis, partners(n, offset))


def params(mib):
    return pltpu.CompilerParams(vmem_limit_bytes=mib << 20)


def project_kernel(n, residual, gain, smooth, w_query, w_keyval, *rest):
    outs = rest[:n]
    x_buf, g_buf, s_buf, q_buf, k_buf, smoothed, q_sum, k_sum, squares_sum, sems, big_sems = rest[n:]
    rows, width = x_buf.shape
    queries = w_query.shape[1]
    steps = big_sems.shape[0] - 1
    depth = width // steps
    small = [
        pltpu.make_async_copy(source, target, sems.at[i])
        for i, (source, target) in enumerate([(residual, x_buf), (gain, g_buf), (smooth, s_buf)])
    ]
    for copy in small:
        copy.start()
    large = []
    for i in range(steps):
        part = pl.ds(i * depth, depth)
        large.append(pltpu.make_async_copy(w_query.at[part], q_buf.at[part], big_sems.at[i]))
    large.append(pltpu.make_async_copy(w_keyval, k_buf, big_sems.at[steps]))
    for copy in large:
        copy.start(priority=1)
    for copy in small:
        copy.wait()
    squares = jnp.zeros((rows, LANES), f32)
    for i in range(width // LANES):
        lanes = slice(i * LANES, (i + 1) * LANES)
        x = x_buf[:, lanes].astype(f32)
        squares += x * x
        smoothed[:, lanes] = (x * (g_buf[i : i + 1, :] / s_buf[i : i + 1, :])).astype(bf16)
    squares_sum[...] = jnp.broadcast_to(jnp.sum(squares, axis=1, keepdims=True), (rows, LANES))
    for i in range(steps):
        part = slice(i * depth, (i + 1) * depth)
        large[i].wait()
        term = jnp.dot(smoothed[:, part], q_buf[part, :], preferred_element_type=f32)
        if i == 0:
            q_sum[...] = term
        else:
            q_sum[...] += term
    large[steps].wait()
    k_sum[...] = jnp.dot(smoothed[...], k_buf[...], preferred_element_type=f32)
    me = lax.axis_index("gx")
    requests = rows // n
    columns = queries + k_buf.shape[1]
    for k in range(n):
        at = pl.ds(pl.multiple_of((me ^ k) * requests, requests), requests)
        outs[k][:, :queries] = q_sum[at, :]
        outs[k][:, queries:columns] = k_sum[at, :]
        outs[k][:, columns:] = squares_sum[at, :]


def project(n, residual, gain, smooth, w_query, w_keyval):
    rows, width = residual.shape
    columns = w_query.shape[1] + w_keyval.shape[1]
    steps = 8
    return pl.pallas_call(
        functools.partial(project_kernel, n),
        in_specs=[HBM] * 5,
        out_specs=[VMEM] * n,
        out_shape=[jax.ShapeDtypeStruct((rows // n, columns + LANES), f32)] * n,
        scratch_shapes=[
            pltpu.VMEM((rows, width), bf16),
            pltpu.VMEM((width // LANES, LANES), f32),
            pltpu.VMEM((width // LANES, LANES), f32),
            pltpu.VMEM(w_query.shape, bf16),
            pltpu.VMEM(w_keyval.shape, bf16),
            pltpu.VMEM((rows, width), bf16),
            pltpu.VMEM((rows, w_query.shape[1]), f32),
            pltpu.VMEM((rows, w_keyval.shape[1]), f32),
            pltpu.VMEM((rows, LANES), f32),
            pltpu.SemaphoreType.DMA((3,)),
            pltpu.SemaphoreType.DMA((steps + 1,)),
        ],
        compiler_params=params(60),
        name="project",
    )(residual, gain.reshape(-1, LANES), smooth.reshape(-1, LANES), w_query, w_keyval)


def norm_kernel(query_scale, keyval_scale, *refs):
    parts, out = refs[:-1], refs[-1]
    total = parts[0][...]
    for part in parts[1:]:
        total = total + part[...]
    columns = out.shape[1]
    row_scale = lax.rsqrt(total[:, columns : columns + 1] / D + EPSILON)
    tiles = query_scale.shape[0]
    for t in range(columns // LANES):
        scale = query_scale[t : t + 1, :] if t < tiles else keyval_scale[t - tiles : t - tiles + 1, :]
        lanes = slice(t * LANES, (t + 1) * LANES)
        out[:, lanes] = (row_scale * (total[:, lanes] * scale)).astype(bf16)


def norm(parts, query_scale, keyval_scale):
    rows, columns = parts[0].shape
    return pl.pallas_call(
        norm_kernel,
        in_specs=[VMEM] * (2 + len(parts)),
        out_specs=VMEM,
        out_shape=jax.ShapeDtypeStruct((rows, columns - LANES), bf16),
        compiler_params=params(8),
        name="norm",
    )(query_scale.reshape(-1, LANES), keyval_scale.reshape(-1, LANES), *parts)


def fetch_kernel(first, _, source, target, sem):
    copy = pltpu.make_async_copy(source.at[pl.ds(first, target.shape[0])], target, sem)
    copy.start()
    copy.wait()


def fetch(after, array, first, count):
    shape = (count,) + array.shape[1:]
    size = count * (array.size // array.shape[0]) * array.dtype.itemsize
    return pl.pallas_call(
        functools.partial(fetch_kernel, first),
        in_specs=[ANY, HBM],
        out_specs=VMEM,
        out_shape=jax.ShapeDtypeStruct(shape, array.dtype),
        scratch_shapes=[pltpu.SemaphoreType.DMA],
        compiler_params=params(40),
        cost_estimate=pl.CostEstimate(flops=0, bytes_accessed=2 * size, transcendentals=0),
        name="fetch",
    )(after, array)


def digits(value, units):
    rows = []
    for unit in units:
        rows.append(jnp.floor(value * (1 / unit) + 0.5))
        value = value - rows[-1] * unit
    return rows + [value]


def joined_digits(rows, units):
    value = rows[0] * units[0]
    for row, unit in zip(rows[1:], units[1:] + (1.0,)):
        value = value + row * unit
    return value


def attend_kernel(n, *refs):
    pieces, refs = refs[: n // 2 + 1], refs[n // 2 + 1 :]
    lengths, keys, values, key_scale, value_scale = refs[:5]
    outs = refs[5 : n + 5]
    placed, q_rows, logits, messages, fresh = refs[n + 5 :]
    requests, _, local, _ = keys.shape
    me = lax.axis_index("gx")
    place(placed, pieces, n)
    queries = HEADS * HEAD_DIM // n
    per = queries // LANES
    for h in range(HEADS):
        tile = placed[h // per, :, (h % per) * LANES : (h % per + 1) * LANES]
        q_rows[pl.ds(h, requests, stride=HEADS), :] = tile
    share = (placed.shape[2] - queries) // LANES
    for c in range(2 * KV_HEADS):
        start = queries + c % share * LANES
        fresh[pl.ds(c, requests, stride=2 * KV_HEADS), :] = placed[c // share, :, start : start + LANES]
    multiplier = HEAD_DIM ** (-0.5)
    for r in range(requests):
        for g in range(KV_HEADS):
            at = slice(r * HEADS + g * GROUP, r * HEADS + (g + 1) * GROUP)
            logits[at, :] = lax.dot_general(
                q_rows[at, :].astype(bf16), keys[r, g], (((1,), (1,)), ((), ())), preferred_element_type=f32
            )
    position = lax.broadcasted_iota(jnp.int32, (GROUP, local), 1) + me * local
    first = me == 0
    count = requests * GROUP
    tops, totals = [[] for _ in range(n)], [[] for _ in range(n)]
    for r in range(requests):
        for g in range(KV_HEADS):
            row = r * HEADS + g * GROUP
            at = slice(row, row + GROUP)
            scale_at = r * KV_HEADS + g
            visible = position < lengths[r]
            scores = logits[at, :] * key_scale[scale_at : scale_at + 1, :] * multiplier
            scores = jnp.where(visible, scores, NEGATIVE)
            new_key = fresh[r * 2 * KV_HEADS + g : r * 2 * KV_HEADS + g + 1, :]
            new_value = fresh[r * 2 * KV_HEADS + KV_HEADS + g : r * 2 * KV_HEADS + KV_HEADS + g + 1, :]
            own = jnp.sum(q_rows[at, :] * new_key, axis=1, keepdims=True) * multiplier
            own = jnp.where(first, own, NEGATIVE)
            top = jnp.maximum(jnp.max(scores, axis=1, keepdims=True), own)
            weights = jnp.where(visible, jnp.exp(scores - top), 0.0)
            own_weight = jnp.where(first, jnp.exp(own - top), 0.0)
            totals[g].append(jnp.sum(weights, axis=1, keepdims=True) + own_weight)
            tops[g].append(top)
            scaled = (weights * value_scale[scale_at : scale_at + 1, :]).astype(bf16)
            mixed = jnp.dot(scaled, values[r, g], preferred_element_type=f32) + own_weight * new_value
            messages[g, r * GROUP : (r + 1) * GROUP, :] = mixed
    diagonal = lax.broadcasted_iota(jnp.int32, (LANES, LANES), 0) == lax.broadcasted_iota(jnp.int32, (LANES, LANES), 1)
    wide = LANES // GROUP
    for p in range(n):
        rows = []
        for b in range(count // LANES):
            top, total = [
                jnp.sum(jnp.where(diagonal, jnp.concatenate(kind[p][b * wide : (b + 1) * wide], axis=0), 0.0), axis=0, keepdims=True)
                for kind in (tops, totals)
            ]
            rows += digits(jnp.maximum(top, LOWEST), UNITS) + digits(total, (1.0,))
        spare = messages.shape[1] - count - len(rows)
        messages[p, count:, :] = jnp.concatenate(rows + [jnp.zeros((spare, LANES), f32)], axis=0)
    for k in range(n):
        outs[k][...] = messages[me ^ k]


def attend(n, pieces, lengths, keys, values, key_scale, value_scale):
    requests, _, local, _ = keys.shape
    count = requests * GROUP
    height = count + -(-(len(UNITS) + 3) * (count // LANES) // 8) * 8
    return pl.pallas_call(
        functools.partial(attend_kernel, n),
        in_specs=[VMEM] * len(pieces) + [SMEM, VMEM, VMEM, VMEM, VMEM],
        out_specs=[VMEM] * n,
        out_shape=[jax.ShapeDtypeStruct((height, LANES), f32)] * n,
        scratch_shapes=[
            pltpu.VMEM((n,) + pieces[0].shape[1:], f32),
            pltpu.VMEM((requests * HEADS, HEAD_DIM), f32),
            pltpu.VMEM((requests * HEADS, local), f32),
            pltpu.VMEM((n, height, LANES), f32),
            pltpu.VMEM((requests * 2 * KV_HEADS, HEAD_DIM), f32),
        ],
        compiler_params=params(24),
        name="attend",
    )(*pieces, lengths, keys, values, key_scale.reshape(-1, local), value_scale.reshape(-1, local))


def merge_kernel(*refs):
    parts, out, mixed = refs[:-2], refs[-2], refs[-1]
    count = mixed.shape[0]
    requests = out.shape[0]
    diagonal = lax.broadcasted_iota(jnp.int32, (LANES, LANES), 0) == lax.broadcasted_iota(jnp.int32, (LANES, LANES), 1)
    blocks = count // LANES
    for b in range(blocks):
        at = slice(b * LANES, (b + 1) * LANES)
        first, size = count + b * (len(UNITS) + 3), len(UNITS) + 1
        rows = [[part[first + i : first + i + 1, :] for i in range(size + 2)] for part in parts]
        tops = [joined_digits(row[:size], UNITS) for row in rows]
        totals = [joined_digits(row[size:], (1.0,)) for row in rows]
        largest = tops[0]
        for top in tops[1:]:
            largest = jnp.maximum(largest, top)
        factors = [jnp.exp(top - largest) for top in tops]
        total = factors[0] * totals[0]
        for factor, other in zip(factors[1:], totals[1:]):
            total = total + factor * other
        sums = None
        for factor, part in zip(factors, parts):
            column = jnp.sum(jnp.where(diagonal, factor, 0.0), axis=1, keepdims=True)
            term = column * part[at, :]
            sums = term if sums is None else sums + term
        column = jnp.sum(jnp.where(diagonal, total, 0.0), axis=1, keepdims=True)
        mixed[at, :] = sums / column
    for h in range(count // requests):
        out[:, h * HEAD_DIM : (h + 1) * HEAD_DIM] = mixed[pl.ds(h, requests, stride=count // requests), :].astype(bf16)


def merge(parts, requests):
    count = requests * GROUP
    return pl.pallas_call(
        merge_kernel,
        in_specs=[VMEM] * len(parts),
        out_specs=VMEM,
        out_shape=jax.ShapeDtypeStruct((requests, GROUP * HEAD_DIM), bf16),
        scratch_shapes=[pltpu.VMEM((count, HEAD_DIM), f32)],
        compiler_params=params(8),
        name="merge",
    )(*parts)


def output_kernel(n, *refs):
    pieces, refs = refs[: n // 2 + 1], refs[n // 2 + 1 :]
    upper, lower, out_scale, ffn, kept, given, total, placed = refs
    head, width = upper.shape
    place(placed, pieces, n)
    attended = placed[...].reshape(total.shape[0], head + lower.shape[0]).astype(bf16)
    span = width // 4
    for i in range(4):
        part = slice(i * span, (i + 1) * span)
        total[:, part] = jnp.dot(attended[:, :head], upper[:, part], preferred_element_type=f32) + jnp.dot(
            attended[:, head:], lower[:, part], preferred_element_type=f32
        )
    for t in range(width // LANES):
        lanes = slice(t * LANES, (t + 1) * LANES)
        total[:, lanes] = total[:, lanes] * out_scale[t : t + 1, :] + ffn[:, lanes]
    rows = total.shape[0] // 2
    core = lax.axis_index("gy") & 1
    kept[...] = total[pl.ds(pl.multiple_of(core * rows, rows), rows), :]
    given[...] = total[pl.ds(pl.multiple_of((1 - core) * rows, rows), rows), :]


def output(pieces, upper, lower, out_scale, ffn):
    n = 2 * (len(pieces) - 1)
    rows, width = ffn.shape
    return pl.pallas_call(
        functools.partial(output_kernel, n),
        in_specs=[VMEM] * (len(pieces) + 4),
        out_specs=[VMEM] * 2,
        out_shape=[jax.ShapeDtypeStruct((rows // 2, width), f32)] * 2,
        scratch_shapes=[pltpu.VMEM((rows, width), f32), pltpu.VMEM((n,) + pieces[0].shape[1:], f32)],
        compiler_params=params(20),
        name="output",
    )(*pieces, upper, lower, out_scale.reshape(-1, LANES), ffn)


def body(n_gx, n_gy, residual, ffn_partial, norm_gain, smooth_scale, w_query, query_scale, w_keyval, keyval_scale,
         key_cache, value_cache, key_scale, value_scale, lengths, w_out, out_scale):
    gy = lax.axis_index("gy")
    rows = residual.shape[0]
    requests = rows // n_gy
    parts = project(n_gx, residual, norm_gain, smooth_scale, w_query, w_keyval)
    head = w_out.shape[0] * 6 // 8
    upper = fetch(parts[0], w_out, 0, head)
    total = trade(parts, "gx", n_gx)
    total[0], upper = lax.optimization_barrier((total[0], upper))
    pieces = spread(norm(total, query_scale, keyval_scale), n_gx)
    parts = attend(n_gx, pieces, lengths, key_cache, value_cache, key_scale, value_scale)
    lower = fetch(parts[0], w_out, head, w_out.shape[0] - head)
    total = trade([part.astype(jnp.float16) for part in parts], "gx", n_gx)
    total = [parts[0]] + [part.astype(f32) for part in total[1:]]
    total[0], lower = lax.optimization_barrier((total[0], lower))
    pieces = spread(merge(total, requests), n_gx)
    kept, given = output(pieces, upper, lower, out_scale, ffn_partial[0])
    core = gy & 1
    chip = kept + swap(given, "gy", n_gy, 1)
    other = swap((chip * (1 / SHRINK)).astype(jnp.float16), "gy", n_gy, 2)
    whole = chip + other.astype(f32) * SHRINK
    mine = lax.dynamic_slice_in_dim(residual, core * (rows // 2), rows // 2, 0)
    mine = (mine.astype(f32) + whole).astype(bf16)
    return jnp.concatenate(ordered([mine, swap(mine, "gy", n_gy, 1)], core))


def joined(value, axis, join):
    pieces = jax.tree.map(lambda part: lax.all_gather(part, axis), value)
    head = jax.tree.map(lambda part: part[0], pieces)
    tail = jax.tree.map(lambda part: part[1:], pieces)
    subtotal, _ = lax.scan(lambda subtotal, piece: (join(subtotal, piece), None), head, tail)
    return subtotal


def combine(former, latter):
    top = jnp.maximum(former[0], latter[0])
    first_factor = jnp.exp(former[0] - top)
    second_factor = jnp.exp(latter[0] - top)
    total = former[1] * first_factor + latter[1] * second_factor
    mixed = former[2] * first_factor[..., None] + latter[2] * second_factor[..., None]
    return (top, total, mixed)


def plain_body(
    residual,
    ffn_partial,
    norm_gain,
    smooth_scale,
    w_query,
    query_scale,
    w_keyval,
    keyval_scale,
    key_cache,
    value_cache,
    key_scale,
    value_scale,
    lengths,
    w_out,
    out_scale,
):
    widened = residual.astype(jnp.float32)
    ffn_total = lax.psum(ffn_partial[0], "gy")
    squares = jnp.sum(widened * widened, axis=1)
    smoothed = (widened * (norm_gain / smooth_scale)).astype(jnp.bfloat16)
    query_part = jnp.dot(smoothed, w_query, preferred_element_type=jnp.float32) * query_scale
    keyval_part = jnp.dot(smoothed, w_keyval, preferred_element_type=jnp.float32) * keyval_scale
    query_sum, keyval_sum, square_sum = lax.psum((query_part, keyval_part, squares), "gx")
    row_scale = lax.rsqrt(square_sum / D + EPSILON)[:, None]
    query_rows = (row_scale * query_sum).astype(jnp.bfloat16)
    keyval_rows = (row_scale * keyval_sum).astype(jnp.bfloat16)
    query_vectors, keyvals = (
        lax.all_to_all(query_rows, "gy", split_axis=0, concat_axis=1, tiled=True),
        lax.all_to_all(keyval_rows, "gy", split_axis=0, concat_axis=1, tiled=True),
    )
    requests = query_vectors.shape[0]
    local = key_cache.shape[2]
    group = HEADS // KV_HEADS
    score_multiplier = HEAD_DIM ** (-0.5)
    grouped = query_vectors.reshape(requests, KV_HEADS, group, HEAD_DIM)
    fresh_key_rows = keyvals[:, : KV_HEADS * HEAD_DIM].reshape(requests, KV_HEADS, HEAD_DIM)
    fresh_value_rows = keyvals[:, KV_HEADS * HEAD_DIM :].reshape(requests, KV_HEADS, HEAD_DIM)
    logit_scores = jnp.einsum(
        "rgqd,rgsd->rgqs", grouped, key_cache, preferred_element_type=jnp.float32
    )
    logit_scores = logit_scores * key_scale[:, :, None, :] * score_multiplier
    position = lax.axis_index("gx") * local + jnp.arange(local, dtype=jnp.int32)
    visible = (position[None, :] < lengths[:, None])[:, None, None, :]
    logit_scores = jnp.where(visible, logit_scores, NEGATIVE)
    local_top = jnp.max(logit_scores, axis=-1)
    weights = jnp.where(visible, jnp.exp(logit_scores - local_top[..., None]), 0.0)
    local_total = jnp.sum(weights, axis=-1)
    scaled = (weights * value_scale[:, :, None, :]).astype(jnp.bfloat16)
    local_mixed = jnp.einsum(
        "rgqs,rgsd->rgqd", scaled, value_cache, preferred_element_type=jnp.float32
    )
    top, total, mixed = joined((local_top, local_total, local_mixed), "gx", combine)
    own = (
        jnp.einsum("rgqd,rgd->rgq", grouped, fresh_key_rows, preferred_element_type=jnp.float32)
        * score_multiplier
    )
    largest = jnp.maximum(top, own)
    old_factor = jnp.exp(top - largest)
    own_weight = jnp.exp(own - largest)
    total = total * old_factor + own_weight
    mixed = (
        mixed * old_factor[..., None]
        + own_weight[..., None] * fresh_value_rows.astype(jnp.float32)[:, :, None, :]
    )
    attended = (mixed / total[..., None]).astype(jnp.bfloat16).reshape(requests, HEADS * HEAD_DIM)
    head_block = lax.all_to_all(attended, "gy", split_axis=1, concat_axis=0, tiled=True)
    projected = jnp.dot(head_block, w_out, preferred_element_type=jnp.float32) * out_scale
    attention_total = lax.psum(projected, "gy")
    new_residual = (widened + ffn_total + attention_total).astype(jnp.bfloat16)
    return new_residual


def solution(mesh):
    placed = (
        P("rep", "gx"), P("gy", "rep", "gx"), P("gx"), P("gx"), P("gx", "gy"), P("gy"), P("gx", "gy"), P("gy"),
        P(("rep", "gy"), None, "gx", None), P(("rep", "gy"), None, "gx", None),
        P(("rep", "gy"), None, "gx"), P(("rep", "gy"), None, "gx"), P(("rep", "gy")), P("gy", "gx"), P("gx"),
    )
    n_gx, n_gy = mesh.shape["gx"], mesh.shape["gy"]

    def run(*arrays):
        if n_gx == 4 and n_gy == 4:
            return body(n_gx, n_gy, *arrays)
        return plain_body(*arrays)

    return jax.shard_map(run, mesh=mesh, in_specs=placed, out_specs=P("rep", "gx"), check_vma=False)
```

```python
import functools

import jax
import jax.numpy as jnp
from jax import lax
from jax.experimental import pallas as pl
from jax.experimental.pallas import tpu as pltpu
from jax.sharding import PartitionSpec as P

D = 16384
HEADS = 64
KV_HEADS = 4
HEAD_DIM = 128
GROUP = HEADS // KV_HEADS
EPSILON = 1e-05
NEGATIVE = -1e30
LANES = 128
LOWEST = -4e7
TOP_UNITS = (32768.0, 16.0, 0.0078125)
TOTAL_UNITS = (1.0, 0.0009765625)
STATISTICS = len(TOP_UNITS) + len(TOTAL_UNITS) + 2
SHRINK = 32.0
f32 = jnp.float32
bf16 = jnp.bfloat16
VMEM = pl.BlockSpec(memory_space=pltpu.VMEM)
SMEM = pl.BlockSpec(memory_space=pltpu.SMEM)
ANY = pl.BlockSpec(memory_space=pl.ANY)
HBM = pl.BlockSpec(memory_space=pltpu.HBM)


def partners(n, offset):
    return [(i, i ^ offset) for i in range(n)]


def ordered(pieces, me):
    n = len(pieces)
    return [lax.select_n(me, *[pieces[j ^ i] for i in range(n)]) for j in range(n)]


def trade(chunks, axis, n):
    return [chunks[0]] + [lax.ppermute(chunks[k], axis, partners(n, k)) for k in [n - 1, *range(1, n - 1)]]


def place(placed, pieces, n):
    gx = lax.axis_index("gx")
    for k in range(n // 2):
        for core in range(2):
            placed[2 * ((gx & 1) ^ k) + core] = pieces[k][core].astype(f32)

    @pl.when((gx == lax.axis_index("gy")) & (gx // 2 == (gx & 1)))
    def _():
        for core in range(2):
            placed[2 * (gx // 2) + core] = pieces[n // 2][core].astype(f32)


def pair_kernel(mine, other, out):
    core = lax.axis_index("gy") & 1
    out[core] = mine[...]
    out[1 - core] = other[...]


def spread(value, n):
    pair = pl.pallas_call(
        pair_kernel,
        in_specs=[VMEM] * 2,
        out_specs=VMEM,
        out_shape=jax.ShapeDtypeStruct((2,) + value.shape, value.dtype),
        compiler_params=params(4),
        name="pair",
    )(value, swap(value, "gy", n, 1))
    pieces = []
    for k in range(n // 2):
        pairs = [(a * n + b, (2 * (b % 2) + ((b // 2) ^ k)) * n + a) for a in range(n) for b in range(n)]
        pieces.append(lax.ppermute(pair, ("gx", "gy"), [p for p in pairs if p[0] != p[1]]))
    return pieces + [pair]


def swap(value, axis, n, offset):
    return lax.ppermute(value, axis, partners(n, offset))


def params(mib):
    return pltpu.CompilerParams(vmem_limit_bytes=mib << 20)


def project_kernel(n, residual, gain, smooth, w_query, w_keyval, *rest):
    outs = rest[:n]
    x_buf, g_buf, s_buf, q_buf, k_buf, smoothed, q_sum, k_sum, squares_sum, sems, big_sems = rest[n:]
    rows, width = x_buf.shape
    queries = w_query.shape[1]
    steps = big_sems.shape[0] - 1
    depth = width // steps
    small = [
        pltpu.make_async_copy(source, target, sems.at[i])
        for i, (source, target) in enumerate([(residual, x_buf), (gain, g_buf), (smooth, s_buf)])
    ]
    for copy in small:
        copy.start()
    large = []
    for i in range(steps):
        part = pl.ds(i * depth, depth)
        large.append(pltpu.make_async_copy(w_query.at[part], q_buf.at[part], big_sems.at[i]))
    large.append(pltpu.make_async_copy(w_keyval, k_buf, big_sems.at[steps]))
    for copy in large:
        copy.start(priority=1)
    for copy in small:
        copy.wait()
    squares = jnp.zeros((rows, LANES), f32)
    for i in range(width // LANES):
        lanes = slice(i * LANES, (i + 1) * LANES)
        x = x_buf[:, lanes].astype(f32)
        squares += x * x
        smoothed[:, lanes] = (x * (g_buf[i : i + 1, :] / s_buf[i : i + 1, :])).astype(bf16)
    squares_sum[...] = jnp.broadcast_to(jnp.sum(squares, axis=1, keepdims=True), (rows, LANES))
    for i in range(steps):
        part = slice(i * depth, (i + 1) * depth)
        large[i].wait()
        term = jnp.dot(smoothed[:, part], q_buf[part, :], preferred_element_type=f32)
        if i == 0:
            q_sum[...] = term
        else:
            q_sum[...] += term
    large[steps].wait()
    k_sum[...] = jnp.dot(smoothed[...], k_buf[...], preferred_element_type=f32)
    me = lax.axis_index("gx")
    requests = rows // n
    columns = queries + k_buf.shape[1]
    for k in range(n):
        at = pl.ds(pl.multiple_of((me ^ k) * requests, requests), requests)
        outs[k][:, :queries] = q_sum[at, :]
        outs[k][:, queries:columns] = k_sum[at, :]
        outs[k][:, columns:] = squares_sum[at, :]


def project(n, residual, gain, smooth, w_query, w_keyval):
    rows, width = residual.shape
    columns = w_query.shape[1] + w_keyval.shape[1]
    steps = 8
    return pl.pallas_call(
        functools.partial(project_kernel, n),
        in_specs=[HBM] * 5,
        out_specs=[VMEM] * n,
        out_shape=[jax.ShapeDtypeStruct((rows // n, columns + LANES), f32)] * n,
        scratch_shapes=[
            pltpu.VMEM((rows, width), bf16),
            pltpu.VMEM((width // LANES, LANES), f32),
            pltpu.VMEM((width // LANES, LANES), f32),
            pltpu.VMEM(w_query.shape, bf16),
            pltpu.VMEM(w_keyval.shape, bf16),
            pltpu.VMEM((rows, width), bf16),
            pltpu.VMEM((rows, w_query.shape[1]), f32),
            pltpu.VMEM((rows, w_keyval.shape[1]), f32),
            pltpu.VMEM((rows, LANES), f32),
            pltpu.SemaphoreType.DMA((3,)),
            pltpu.SemaphoreType.DMA((steps + 1,)),
        ],
        compiler_params=params(60),
        name="project",
    )(residual, gain.reshape(-1, LANES), smooth.reshape(-1, LANES), w_query, w_keyval)


def norm_kernel(query_scale, keyval_scale, *refs):
    parts, out = refs[:-1], refs[-1]
    total = parts[0][...]
    for part in parts[1:]:
        total = total + part[...]
    columns = out.shape[1]
    row_scale = lax.rsqrt(total[:, columns : columns + 1] / D + EPSILON)
    tiles = query_scale.shape[0]
    for t in range(columns // LANES):
        scale = query_scale[t : t + 1, :] if t < tiles else keyval_scale[t - tiles : t - tiles + 1, :]
        lanes = slice(t * LANES, (t + 1) * LANES)
        out[:, lanes] = (row_scale * (total[:, lanes] * scale)).astype(bf16)


def norm(parts, query_scale, keyval_scale):
    rows, columns = parts[0].shape
    return pl.pallas_call(
        norm_kernel,
        in_specs=[VMEM] * (2 + len(parts)),
        out_specs=VMEM,
        out_shape=jax.ShapeDtypeStruct((rows, columns - LANES), bf16),
        compiler_params=params(8),
        name="norm",
    )(query_scale.reshape(-1, LANES), keyval_scale.reshape(-1, LANES), *parts)


def fetch_kernel(first, _, source, target, sem):
    copy = pltpu.make_async_copy(source.at[pl.ds(first, target.shape[0])], target, sem)
    copy.start()
    copy.wait()


def fetch(after, array, first, count):
    shape = (count,) + array.shape[1:]
    size = count * (array.size // array.shape[0]) * array.dtype.itemsize
    return pl.pallas_call(
        functools.partial(fetch_kernel, first),
        in_specs=[ANY, HBM],
        out_specs=VMEM,
        out_shape=jax.ShapeDtypeStruct(shape, array.dtype),
        scratch_shapes=[pltpu.SemaphoreType.DMA],
        compiler_params=params(40),
        cost_estimate=pl.CostEstimate(flops=0, bytes_accessed=2 * size, transcendentals=0),
        name="fetch",
    )(after, array)


def digits(value, units):
    rows = []
    for unit in units:
        rows.append(jnp.floor(value * (1 / unit) + 0.5))
        value = value - rows[-1] * unit
    return rows + [value]


def joined_digits(rows, units):
    value = rows[0] * units[0]
    for row, unit in zip(rows[1:], units[1:] + (1.0,)):
        value = value + row * unit
    return value


def attend_kernel(n, *refs):
    pieces, refs = refs[: n // 2 + 1], refs[n // 2 + 1 :]
    lengths, keys, values, key_scale, value_scale = refs[:5]
    outs = refs[5 : n + 5]
    placed, q_rows, logits, messages, fresh = refs[n + 5 :]
    requests, _, local, _ = keys.shape
    me = lax.axis_index("gx")
    place(placed, pieces, n)
    queries = HEADS * HEAD_DIM // n
    per = queries // LANES
    for h in range(HEADS):
        tile = placed[h // per, :, (h % per) * LANES : (h % per + 1) * LANES]
        q_rows[pl.ds(h, requests, stride=HEADS), :] = tile
    share = (placed.shape[2] - queries) // LANES
    for c in range(2 * KV_HEADS):
        start = queries + c % share * LANES
        fresh[pl.ds(c, requests, stride=2 * KV_HEADS), :] = placed[c // share, :, start : start + LANES]
    multiplier = HEAD_DIM ** (-0.5)
    for r in range(requests):
        for g in range(KV_HEADS):
            at = slice(r * HEADS + g * GROUP, r * HEADS + (g + 1) * GROUP)
            logits[at, :] = lax.dot_general(
                q_rows[at, :].astype(bf16), keys[r, g], (((1,), (1,)), ((), ())), preferred_element_type=f32
            )
    position = lax.broadcasted_iota(jnp.int32, (GROUP, local), 1) + me * local
    first = me == 0
    count = requests * GROUP
    tops, totals = [[] for _ in range(n)], [[] for _ in range(n)]
    for r in range(requests):
        for g in range(KV_HEADS):
            row = r * HEADS + g * GROUP
            at = slice(row, row + GROUP)
            scale_at = r * KV_HEADS + g
            visible = position < lengths[r]
            scores = logits[at, :] * key_scale[scale_at : scale_at + 1, :] * multiplier
            scores = jnp.where(visible, scores, NEGATIVE)
            new_key = fresh[r * 2 * KV_HEADS + g : r * 2 * KV_HEADS + g + 1, :]
            new_value = fresh[r * 2 * KV_HEADS + KV_HEADS + g : r * 2 * KV_HEADS + KV_HEADS + g + 1, :]
            own = jnp.sum(q_rows[at, :] * new_key, axis=1, keepdims=True) * multiplier
            own = jnp.where(first, own, NEGATIVE)
            top = jnp.maximum(jnp.max(scores, axis=1, keepdims=True), own)
            weights = jnp.where(visible, jnp.exp(scores - top), 0.0)
            own_weight = jnp.where(first, jnp.exp(own - top), 0.0)
            totals[g].append(jnp.sum(weights, axis=1, keepdims=True) + own_weight)
            tops[g].append(top)
            scaled = (weights * value_scale[scale_at : scale_at + 1, :]).astype(bf16)
            mixed = jnp.dot(scaled, values[r, g], preferred_element_type=f32) + own_weight * new_value
            messages[g, r * GROUP : (r + 1) * GROUP, :] = mixed
    diagonal = lax.broadcasted_iota(jnp.int32, (LANES, LANES), 0) == lax.broadcasted_iota(jnp.int32, (LANES, LANES), 1)
    wide = LANES // GROUP
    for p in range(n):
        rows = []
        for b in range(count // LANES):
            top, total = [
                jnp.sum(jnp.where(diagonal, jnp.concatenate(kind[p][b * wide : (b + 1) * wide], axis=0), 0.0), axis=0, keepdims=True)
                for kind in (tops, totals)
            ]
            rows += digits(jnp.maximum(top, LOWEST), TOP_UNITS) + digits(total, TOTAL_UNITS)
        spare = messages.shape[1] - count - len(rows)
        messages[p, count:, :] = jnp.concatenate(rows + [jnp.zeros((spare, LANES), f32)], axis=0)
    for k in range(n):
        outs[k][...] = messages[me ^ k]


def attend(n, pieces, lengths, keys, values, key_scale, value_scale):
    requests, _, local, _ = keys.shape
    count = requests * GROUP
    height = count + -(-STATISTICS * (count // LANES) // 8) * 8
    return pl.pallas_call(
        functools.partial(attend_kernel, n),
        in_specs=[VMEM] * len(pieces) + [SMEM, VMEM, VMEM, VMEM, VMEM],
        out_specs=[VMEM] * n,
        out_shape=[jax.ShapeDtypeStruct((height, LANES), f32)] * n,
        scratch_shapes=[
            pltpu.VMEM((n,) + pieces[0].shape[1:], f32),
            pltpu.VMEM((requests * HEADS, HEAD_DIM), f32),
            pltpu.VMEM((requests * HEADS, local), f32),
            pltpu.VMEM((n, height, LANES), f32),
            pltpu.VMEM((requests * 2 * KV_HEADS, HEAD_DIM), f32),
        ],
        compiler_params=params(24),
        name="attend",
    )(*pieces, lengths, keys, values, key_scale.reshape(-1, local), value_scale.reshape(-1, local))


def merge_kernel(*refs):
    parts, out, mixed = refs[:-2], refs[-2], refs[-1]
    count = mixed.shape[0]
    requests = out.shape[0]
    diagonal = lax.broadcasted_iota(jnp.int32, (LANES, LANES), 0) == lax.broadcasted_iota(jnp.int32, (LANES, LANES), 1)
    blocks = count // LANES
    for b in range(blocks):
        at = slice(b * LANES, (b + 1) * LANES)
        first, size = count + b * STATISTICS, len(TOP_UNITS) + 1
        rows = [[part[first + i : first + i + 1, :] for i in range(STATISTICS)] for part in parts]
        tops = [joined_digits(row[:size], TOP_UNITS) for row in rows]
        totals = [joined_digits(row[size:], TOTAL_UNITS) for row in rows]
        largest = tops[0]
        for top in tops[1:]:
            largest = jnp.maximum(largest, top)
        factors = [jnp.exp(top - largest) for top in tops]
        total = factors[0] * totals[0]
        for factor, other in zip(factors[1:], totals[1:]):
            total = total + factor * other
        sums = None
        for factor, part in zip(factors, parts):
            column = jnp.sum(jnp.where(diagonal, factor, 0.0), axis=1, keepdims=True)
            term = column * part[at, :]
            sums = term if sums is None else sums + term
        column = jnp.sum(jnp.where(diagonal, total, 0.0), axis=1, keepdims=True)
        mixed[at, :] = sums / column
    for h in range(count // requests):
        out[:, h * HEAD_DIM : (h + 1) * HEAD_DIM] = mixed[pl.ds(h, requests, stride=count // requests), :].astype(bf16)


def merge(parts, requests):
    count = requests * GROUP
    return pl.pallas_call(
        merge_kernel,
        in_specs=[VMEM] * len(parts),
        out_specs=VMEM,
        out_shape=jax.ShapeDtypeStruct((requests, GROUP * HEAD_DIM), bf16),
        scratch_shapes=[pltpu.VMEM((count, HEAD_DIM), f32)],
        compiler_params=params(8),
        name="merge",
    )(*parts)


def output_kernel(n, *refs):
    pieces, refs = refs[: n // 2 + 1], refs[n // 2 + 1 :]
    upper, lower, out_scale, ffn, kept, given, total, placed = refs
    head, width = upper.shape
    place(placed, pieces, n)
    attended = placed[...].reshape(total.shape[0], head + lower.shape[0]).astype(bf16)
    span = width // 4
    for i in range(4):
        part = slice(i * span, (i + 1) * span)
        total[:, part] = jnp.dot(attended[:, :head], upper[:, part], preferred_element_type=f32) + jnp.dot(
            attended[:, head:], lower[:, part], preferred_element_type=f32
        )
    for t in range(width // LANES):
        lanes = slice(t * LANES, (t + 1) * LANES)
        total[:, lanes] = total[:, lanes] * out_scale[t : t + 1, :] + ffn[:, lanes]
    rows = total.shape[0] // 2
    core = lax.axis_index("gy") & 1
    kept[...] = total[pl.ds(pl.multiple_of(core * rows, rows), rows), :]
    given[...] = total[pl.ds(pl.multiple_of((1 - core) * rows, rows), rows), :]


def output(pieces, upper, lower, out_scale, ffn):
    n = 2 * (len(pieces) - 1)
    rows, width = ffn.shape
    return pl.pallas_call(
        functools.partial(output_kernel, n),
        in_specs=[VMEM] * (len(pieces) + 4),
        out_specs=[VMEM] * 2,
        out_shape=[jax.ShapeDtypeStruct((rows // 2, width), f32)] * 2,
        scratch_shapes=[pltpu.VMEM((rows, width), f32), pltpu.VMEM((n,) + pieces[0].shape[1:], f32)],
        compiler_params=params(20),
        name="output",
    )(*pieces, upper, lower, out_scale.reshape(-1, LANES), ffn)


def body(n_gx, n_gy, residual, ffn_partial, norm_gain, smooth_scale, w_query, query_scale, w_keyval, keyval_scale,
         key_cache, value_cache, key_scale, value_scale, lengths, w_out, out_scale):
    gy = lax.axis_index("gy")
    rows = residual.shape[0]
    requests = rows // n_gy
    parts = project(n_gx, residual, norm_gain, smooth_scale, w_query, w_keyval)
    head = w_out.shape[0] * 11 // 16
    upper = fetch(parts[0], w_out, 0, head)
    total = trade(parts, "gx", n_gx)
    total[0], upper = lax.optimization_barrier((total[0], upper))
    pieces = spread(norm(total, query_scale, keyval_scale), n_gx)
    parts = attend(n_gx, pieces, lengths, key_cache, value_cache, key_scale, value_scale)
    lower = fetch(parts[0], w_out, head, w_out.shape[0] - head)
    total = trade([part.astype(jnp.float16) for part in parts], "gx", n_gx)
    total = [parts[0]] + [part.astype(f32) for part in total[1:]]
    total[0], lower = lax.optimization_barrier((total[0], lower))
    pieces = spread(merge(total, requests), n_gx)
    kept, given = output(pieces, upper, lower, out_scale, ffn_partial[0])
    core = gy & 1
    chip = kept + swap(given, "gy", n_gy, 1)
    other = swap((chip * (1 / SHRINK)).astype(jnp.float16), "gy", n_gy, 2)
    whole = chip + other.astype(f32) * SHRINK
    mine = lax.dynamic_slice_in_dim(residual, core * (rows // 2), rows // 2, 0)
    mine = (mine.astype(f32) + whole).astype(bf16)
    return jnp.concatenate(ordered([mine, swap(mine, "gy", n_gy, 1)], core))


def joined(value, axis, join):
    pieces = jax.tree.map(lambda part: lax.all_gather(part, axis), value)
    head = jax.tree.map(lambda part: part[0], pieces)
    tail = jax.tree.map(lambda part: part[1:], pieces)
    subtotal, _ = lax.scan(lambda subtotal, piece: (join(subtotal, piece), None), head, tail)
    return subtotal


def combine(former, latter):
    top = jnp.maximum(former[0], latter[0])
    first_factor = jnp.exp(former[0] - top)
    second_factor = jnp.exp(latter[0] - top)
    total = former[1] * first_factor + latter[1] * second_factor
    mixed = former[2] * first_factor[..., None] + latter[2] * second_factor[..., None]
    return (top, total, mixed)


def plain_body(
    residual,
    ffn_partial,
    norm_gain,
    smooth_scale,
    w_query,
    query_scale,
    w_keyval,
    keyval_scale,
    key_cache,
    value_cache,
    key_scale,
    value_scale,
    lengths,
    w_out,
    out_scale,
):
    widened = residual.astype(jnp.float32)
    ffn_total = lax.psum(ffn_partial[0], "gy")
    squares = jnp.sum(widened * widened, axis=1)
    smoothed = (widened * (norm_gain / smooth_scale)).astype(jnp.bfloat16)
    query_part = jnp.dot(smoothed, w_query, preferred_element_type=jnp.float32) * query_scale
    keyval_part = jnp.dot(smoothed, w_keyval, preferred_element_type=jnp.float32) * keyval_scale
    query_sum, keyval_sum, square_sum = lax.psum((query_part, keyval_part, squares), "gx")
    row_scale = lax.rsqrt(square_sum / D + EPSILON)[:, None]
    query_rows = (row_scale * query_sum).astype(jnp.bfloat16)
    keyval_rows = (row_scale * keyval_sum).astype(jnp.bfloat16)
    query_vectors, keyvals = (
        lax.all_to_all(query_rows, "gy", split_axis=0, concat_axis=1, tiled=True),
        lax.all_to_all(keyval_rows, "gy", split_axis=0, concat_axis=1, tiled=True),
    )
    requests = query_vectors.shape[0]
    local = key_cache.shape[2]
    group = HEADS // KV_HEADS
    score_multiplier = HEAD_DIM ** (-0.5)
    grouped = query_vectors.reshape(requests, KV_HEADS, group, HEAD_DIM)
    fresh_key_rows = keyvals[:, : KV_HEADS * HEAD_DIM].reshape(requests, KV_HEADS, HEAD_DIM)
    fresh_value_rows = keyvals[:, KV_HEADS * HEAD_DIM :].reshape(requests, KV_HEADS, HEAD_DIM)
    logit_scores = jnp.einsum(
        "rgqd,rgsd->rgqs", grouped, key_cache, preferred_element_type=jnp.float32
    )
    logit_scores = logit_scores * key_scale[:, :, None, :] * score_multiplier
    position = lax.axis_index("gx") * local + jnp.arange(local, dtype=jnp.int32)
    visible = (position[None, :] < lengths[:, None])[:, None, None, :]
    logit_scores = jnp.where(visible, logit_scores, NEGATIVE)
    local_top = jnp.max(logit_scores, axis=-1)
    weights = jnp.where(visible, jnp.exp(logit_scores - local_top[..., None]), 0.0)
    local_total = jnp.sum(weights, axis=-1)
    scaled = (weights * value_scale[:, :, None, :]).astype(jnp.bfloat16)
    local_mixed = jnp.einsum(
        "rgqs,rgsd->rgqd", scaled, value_cache, preferred_element_type=jnp.float32
    )
    top, total, mixed = joined((local_top, local_total, local_mixed), "gx", combine)
    own = (
        jnp.einsum("rgqd,rgd->rgq", grouped, fresh_key_rows, preferred_element_type=jnp.float32)
        * score_multiplier
    )
    largest = jnp.maximum(top, own)
    old_factor = jnp.exp(top - largest)
    own_weight = jnp.exp(own - largest)
    total = total * old_factor + own_weight
    mixed = (
        mixed * old_factor[..., None]
        + own_weight[..., None] * fresh_value_rows.astype(jnp.float32)[:, :, None, :]
    )
    attended = (mixed / total[..., None]).astype(jnp.bfloat16).reshape(requests, HEADS * HEAD_DIM)
    head_block = lax.all_to_all(attended, "gy", split_axis=1, concat_axis=0, tiled=True)
    projected = jnp.dot(head_block, w_out, preferred_element_type=jnp.float32) * out_scale
    attention_total = lax.psum(projected, "gy")
    new_residual = (widened + ffn_total + attention_total).astype(jnp.bfloat16)
    return new_residual


def solution(mesh):
    placed = (
        P("rep", "gx"), P("gy", "rep", "gx"), P("gx"), P("gx"), P("gx", "gy"), P("gy"), P("gx", "gy"), P("gy"),
        P(("rep", "gy"), None, "gx", None), P(("rep", "gy"), None, "gx", None),
        P(("rep", "gy"), None, "gx"), P(("rep", "gy"), None, "gx"), P(("rep", "gy")), P("gy", "gx"), P("gx"),
    )
    n_gx, n_gy = mesh.shape["gx"], mesh.shape["gy"]

    def run(*arrays):
        if n_gx == 4 and n_gy == 4:
            return body(n_gx, n_gy, *arrays)
        return plain_body(*arrays)

    return jax.shard_map(run, mesh=mesh, in_specs=placed, out_specs=P("rep", "gx"), check_vma=False)
```

```python
import functools

import jax
import jax.numpy as jnp
from jax import lax
from jax.experimental import pallas as pl
from jax.experimental.pallas import tpu as pltpu
from jax.sharding import PartitionSpec as P

D = 16384
HEADS = 64
KV_HEADS = 4
HEAD_DIM = 128
GROUP = HEADS // KV_HEADS
EPSILON = 1e-05
NEGATIVE = -1e30
LANES = 128
LOWEST = -4e7
TOP_UNITS = (32768.0, 16.0, 0.0078125)
TOTAL_UNITS = (1.0, 0.0009765625)
STATISTICS = len(TOP_UNITS) + len(TOTAL_UNITS) + 2
PORTIONS = (3, 3, 3, 3, 2, 1, 1)
SHRINK = 32.0
f32 = jnp.float32
bf16 = jnp.bfloat16
VMEM = pl.BlockSpec(memory_space=pltpu.VMEM)
SMEM = pl.BlockSpec(memory_space=pltpu.SMEM)
ANY = pl.BlockSpec(memory_space=pl.ANY)
HBM = pl.BlockSpec(memory_space=pltpu.HBM)


def partners(n, offset):
    return [(i, i ^ offset) for i in range(n)]


def ordered(pieces, me):
    n = len(pieces)
    return [lax.select_n(me, *[pieces[j ^ i] for i in range(n)]) for j in range(n)]


def trade(chunks, axis, n):
    return [chunks[0]] + [lax.ppermute(chunks[k], axis, partners(n, k)) for k in [n - 1, *range(1, n - 1)]]


def place(placed, pieces, n):
    gx = lax.axis_index("gx")
    for k in range(n // 2):
        for core in range(2):
            placed[2 * ((gx & 1) ^ k) + core] = pieces[k][core].astype(f32)

    @pl.when((gx == lax.axis_index("gy")) & (gx // 2 == (gx & 1)))
    def _():
        for core in range(2):
            placed[2 * (gx // 2) + core] = pieces[n // 2][core].astype(f32)


def pair_kernel(mine, other, out):
    core = lax.axis_index("gy") & 1
    out[core] = mine[...]
    out[1 - core] = other[...]


def spread(value, n):
    pair = pl.pallas_call(
        pair_kernel,
        in_specs=[VMEM] * 2,
        out_specs=VMEM,
        out_shape=jax.ShapeDtypeStruct((2,) + value.shape, value.dtype),
        compiler_params=params(4),
        name="pair",
    )(value, swap(value, "gy", n, 1))
    pieces = []
    for k in range(n // 2):
        pairs = [(a * n + b, (2 * (b % 2) + ((b // 2) ^ k)) * n + a) for a in range(n) for b in range(n)]
        pieces.append(lax.ppermute(pair, ("gx", "gy"), [p for p in pairs if p[0] != p[1]]))
    return pieces + [pair]


def swap(value, axis, n, offset):
    return lax.ppermute(value, axis, partners(n, offset))


def params(mib):
    return pltpu.CompilerParams(vmem_limit_bytes=mib << 20)


def project_kernel(n, residual, gain, smooth, w_query, w_keyval, *rest):
    outs = rest[:n]
    x_buf, g_buf, s_buf, q_buf, k_buf, smoothed, q_sum, k_sum, squares_sum, sems, big_sems = rest[n:]
    rows, width = x_buf.shape
    queries = w_query.shape[1]
    steps = len(PORTIONS)
    ends = [sum(PORTIONS[: i + 1]) * width // sum(PORTIONS) for i in range(steps)]
    starts = [0] + ends[:-1]
    small = [
        pltpu.make_async_copy(source, target, sems.at[i])
        for i, (source, target) in enumerate([(residual, x_buf), (gain, g_buf), (smooth, s_buf)])
    ]
    for copy in small:
        copy.start()
    large = []
    for i in range(steps):
        part = pl.ds(starts[i], ends[i] - starts[i])
        large.append(pltpu.make_async_copy(w_query.at[part], q_buf.at[part], big_sems.at[i]))
    weights = pltpu.make_async_copy(w_keyval, k_buf, big_sems.at[steps])
    for copy in large[:2] + [weights] + large[2:]:
        copy.start(priority=1)
    for copy in small:
        copy.wait()
    squares = jnp.zeros((rows, LANES), f32)
    for i in range(width // LANES):
        lanes = slice(i * LANES, (i + 1) * LANES)
        x = x_buf[:, lanes].astype(f32)
        squares += x * x
        smoothed[:, lanes] = (x * (g_buf[i : i + 1, :] / s_buf[i : i + 1, :])).astype(bf16)
    squares_sum[...] = jnp.broadcast_to(jnp.sum(squares, axis=1, keepdims=True), (rows, LANES))
    for i in range(steps):
        part = slice(starts[i], ends[i])
        if i == 2:
            weights.wait()
            k_sum[...] = jnp.dot(smoothed[...], k_buf[...], preferred_element_type=f32)
        large[i].wait()
        term = jnp.dot(smoothed[:, part], q_buf[part, :], preferred_element_type=f32)
        if i == 0:
            q_sum[...] = term
        else:
            q_sum[...] += term
    me = lax.axis_index("gx")
    requests = rows // n
    columns = queries + k_buf.shape[1]
    for k in range(n):
        at = pl.ds(pl.multiple_of((me ^ k) * requests, requests), requests)
        outs[k][:, :queries] = q_sum[at, :]
        outs[k][:, queries:columns] = k_sum[at, :]
        outs[k][:, columns:] = squares_sum[at, :]


def project(n, residual, gain, smooth, w_query, w_keyval):
    rows, width = residual.shape
    columns = w_query.shape[1] + w_keyval.shape[1]
    steps = len(PORTIONS)
    return pl.pallas_call(
        functools.partial(project_kernel, n),
        in_specs=[HBM] * 5,
        out_specs=[VMEM] * n,
        out_shape=[jax.ShapeDtypeStruct((rows // n, columns + LANES), f32)] * n,
        scratch_shapes=[
            pltpu.VMEM((rows, width), bf16),
            pltpu.VMEM((width // LANES, LANES), f32),
            pltpu.VMEM((width // LANES, LANES), f32),
            pltpu.VMEM(w_query.shape, bf16),
            pltpu.VMEM(w_keyval.shape, bf16),
            pltpu.VMEM((rows, width), bf16),
            pltpu.VMEM((rows, w_query.shape[1]), f32),
            pltpu.VMEM((rows, w_keyval.shape[1]), f32),
            pltpu.VMEM((rows, LANES), f32),
            pltpu.SemaphoreType.DMA((3,)),
            pltpu.SemaphoreType.DMA((steps + 1,)),
        ],
        compiler_params=params(60),
        name="project",
    )(residual, gain.reshape(-1, LANES), smooth.reshape(-1, LANES), w_query, w_keyval)


def norm_kernel(query_scale, keyval_scale, *refs):
    parts, out = refs[:-1], refs[-1]
    total = parts[0][...]
    for part in parts[1:]:
        total = total + part[...]
    columns = out.shape[1]
    row_scale = lax.rsqrt(total[:, columns : columns + 1] / D + EPSILON)
    tiles = query_scale.shape[0]
    for t in range(columns // LANES):
        scale = query_scale[t : t + 1, :] if t < tiles else keyval_scale[t - tiles : t - tiles + 1, :]
        lanes = slice(t * LANES, (t + 1) * LANES)
        out[:, lanes] = (row_scale * (total[:, lanes] * scale)).astype(bf16)


def norm(parts, query_scale, keyval_scale):
    rows, columns = parts[0].shape
    return pl.pallas_call(
        norm_kernel,
        in_specs=[VMEM] * (2 + len(parts)),
        out_specs=VMEM,
        out_shape=jax.ShapeDtypeStruct((rows, columns - LANES), bf16),
        compiler_params=params(8),
        name="norm",
    )(query_scale.reshape(-1, LANES), keyval_scale.reshape(-1, LANES), *parts)


def fetch_kernel(first, _, source, target, sem):
    copy = pltpu.make_async_copy(source.at[pl.ds(first, target.shape[0])], target, sem)
    copy.start()
    copy.wait()


def fetch(after, array, first, count):
    shape = (count,) + array.shape[1:]
    size = count * (array.size // array.shape[0]) * array.dtype.itemsize
    return pl.pallas_call(
        functools.partial(fetch_kernel, first),
        in_specs=[ANY, HBM],
        out_specs=VMEM,
        out_shape=jax.ShapeDtypeStruct(shape, array.dtype),
        scratch_shapes=[pltpu.SemaphoreType.DMA],
        compiler_params=params(40),
        cost_estimate=pl.CostEstimate(flops=0, bytes_accessed=2 * size, transcendentals=0),
        name="fetch",
    )(after, array)


def digits(value, units):
    rows = []
    for unit in units:
        rows.append(jnp.floor(value * (1 / unit) + 0.5))
        value = value - rows[-1] * unit
    return rows + [value]


def joined_digits(rows, units):
    value = rows[0] * units[0]
    for row, unit in zip(rows[1:], units[1:] + (1.0,)):
        value = value + row * unit
    return value


def attend_kernel(n, *refs):
    pieces, refs = refs[: n // 2 + 1], refs[n // 2 + 1 :]
    lengths, keys, values, key_scale, value_scale = refs[:5]
    outs = refs[5 : n + 5]
    placed, q_rows, logits, messages, fresh = refs[n + 5 :]
    requests, _, local, _ = keys.shape
    me = lax.axis_index("gx")
    place(placed, pieces, n)
    queries = HEADS * HEAD_DIM // n
    per = queries // LANES
    for h in range(HEADS):
        tile = placed[h // per, :, (h % per) * LANES : (h % per + 1) * LANES]
        q_rows[pl.ds(h, requests, stride=HEADS), :] = tile
    share = (placed.shape[2] - queries) // LANES
    for c in range(2 * KV_HEADS):
        start = queries + c % share * LANES
        fresh[pl.ds(c, requests, stride=2 * KV_HEADS), :] = placed[c // share, :, start : start + LANES]
    multiplier = HEAD_DIM ** (-0.5)
    for r in range(requests):
        for g in range(KV_HEADS):
            at = slice(r * HEADS + g * GROUP, r * HEADS + (g + 1) * GROUP)
            logits[at, :] = lax.dot_general(
                q_rows[at, :].astype(bf16), keys[r, g], (((1,), (1,)), ((), ())), preferred_element_type=f32
            )
    position = lax.broadcasted_iota(jnp.int32, (GROUP, local), 1) + me * local
    first = me == 0
    count = requests * GROUP
    tops, totals = [[] for _ in range(n)], [[] for _ in range(n)]
    for r in range(requests):
        for g in range(KV_HEADS):
            row = r * HEADS + g * GROUP
            at = slice(row, row + GROUP)
            scale_at = r * KV_HEADS + g
            visible = position < lengths[r]
            scores = logits[at, :] * key_scale[scale_at : scale_at + 1, :] * multiplier
            scores = jnp.where(visible, scores, NEGATIVE)
            new_key = fresh[r * 2 * KV_HEADS + g : r * 2 * KV_HEADS + g + 1, :]
            new_value = fresh[r * 2 * KV_HEADS + KV_HEADS + g : r * 2 * KV_HEADS + KV_HEADS + g + 1, :]
            own = jnp.sum(q_rows[at, :] * new_key, axis=1, keepdims=True) * multiplier
            own = jnp.where(first, own, NEGATIVE)
            top = jnp.maximum(jnp.max(scores, axis=1, keepdims=True), own)
            weights = jnp.where(visible, jnp.exp(scores - top), 0.0)
            own_weight = jnp.where(first, jnp.exp(own - top), 0.0)
            totals[g].append(jnp.sum(weights, axis=1, keepdims=True) + own_weight)
            tops[g].append(top)
            scaled = (weights * value_scale[scale_at : scale_at + 1, :]).astype(bf16)
            mixed = jnp.dot(scaled, values[r, g], preferred_element_type=f32) + own_weight * new_value
            messages[g, r * GROUP : (r + 1) * GROUP, :] = mixed
    diagonal = lax.broadcasted_iota(jnp.int32, (LANES, LANES), 0) == lax.broadcasted_iota(jnp.int32, (LANES, LANES), 1)
    wide = LANES // GROUP
    for p in range(n):
        rows = []
        for b in range(count // LANES):
            top, total = [
                jnp.sum(jnp.where(diagonal, jnp.concatenate(kind[p][b * wide : (b + 1) * wide], axis=0), 0.0), axis=0, keepdims=True)
                for kind in (tops, totals)
            ]
            rows += digits(jnp.maximum(top, LOWEST), TOP_UNITS) + digits(total, TOTAL_UNITS)
        spare = messages.shape[1] - count - len(rows)
        messages[p, count:, :] = jnp.concatenate(rows + [jnp.zeros((spare, LANES), f32)], axis=0)
    for k in range(n):
        outs[k][...] = messages[me ^ k]


def attend(n, pieces, lengths, keys, values, key_scale, value_scale):
    requests, _, local, _ = keys.shape
    count = requests * GROUP
    height = count + -(-STATISTICS * (count // LANES) // 8) * 8
    return pl.pallas_call(
        functools.partial(attend_kernel, n),
        in_specs=[VMEM] * len(pieces) + [SMEM, VMEM, VMEM, VMEM, VMEM],
        out_specs=[VMEM] * n,
        out_shape=[jax.ShapeDtypeStruct((height, LANES), f32)] * n,
        scratch_shapes=[
            pltpu.VMEM((n,) + pieces[0].shape[1:], f32),
            pltpu.VMEM((requests * HEADS, HEAD_DIM), f32),
            pltpu.VMEM((requests * HEADS, local), f32),
            pltpu.VMEM((n, height, LANES), f32),
            pltpu.VMEM((requests * 2 * KV_HEADS, HEAD_DIM), f32),
        ],
        compiler_params=params(24),
        name="attend",
    )(*pieces, lengths, keys, values, key_scale.reshape(-1, local), value_scale.reshape(-1, local))


def merge_kernel(*refs):
    parts, out, mixed = refs[:-2], refs[-2], refs[-1]
    count = mixed.shape[0]
    requests = out.shape[0]
    diagonal = lax.broadcasted_iota(jnp.int32, (LANES, LANES), 0) == lax.broadcasted_iota(jnp.int32, (LANES, LANES), 1)
    blocks = count // LANES
    for b in range(blocks):
        at = slice(b * LANES, (b + 1) * LANES)
        first, size = count + b * STATISTICS, len(TOP_UNITS) + 1
        rows = [[part[first + i : first + i + 1, :] for i in range(STATISTICS)] for part in parts]
        tops = [joined_digits(row[:size], TOP_UNITS) for row in rows]
        totals = [joined_digits(row[size:], TOTAL_UNITS) for row in rows]
        largest = tops[0]
        for top in tops[1:]:
            largest = jnp.maximum(largest, top)
        factors = [jnp.exp(top - largest) for top in tops]
        total = factors[0] * totals[0]
        for factor, other in zip(factors[1:], totals[1:]):
            total = total + factor * other
        sums = None
        for factor, part in zip(factors, parts):
            column = jnp.sum(jnp.where(diagonal, factor, 0.0), axis=1, keepdims=True)
            term = column * part[at, :]
            sums = term if sums is None else sums + term
        column = jnp.sum(jnp.where(diagonal, total, 0.0), axis=1, keepdims=True)
        mixed[at, :] = sums / column
    for h in range(count // requests):
        out[:, h * HEAD_DIM : (h + 1) * HEAD_DIM] = mixed[pl.ds(h, requests, stride=count // requests), :].astype(bf16)


def merge(parts, requests):
    count = requests * GROUP
    return pl.pallas_call(
        merge_kernel,
        in_specs=[VMEM] * len(parts),
        out_specs=VMEM,
        out_shape=jax.ShapeDtypeStruct((requests, GROUP * HEAD_DIM), bf16),
        scratch_shapes=[pltpu.VMEM((count, HEAD_DIM), f32)],
        compiler_params=params(8),
        name="merge",
    )(*parts)


def output_kernel(n, *refs):
    pieces, refs = refs[: n // 2 + 1], refs[n // 2 + 1 :]
    upper, lower, out_scale, ffn, kept, given, total, placed = refs
    head, width = upper.shape
    place(placed, pieces, n)
    attended = placed[...].reshape(total.shape[0], head + lower.shape[0]).astype(bf16)
    span = width // 4
    for i in range(4):
        part = slice(i * span, (i + 1) * span)
        total[:, part] = jnp.dot(attended[:, :head], upper[:, part], preferred_element_type=f32) + jnp.dot(
            attended[:, head:], lower[:, part], preferred_element_type=f32
        )
    for t in range(width // LANES):
        lanes = slice(t * LANES, (t + 1) * LANES)
        total[:, lanes] = total[:, lanes] * out_scale[t : t + 1, :] + ffn[:, lanes]
    rows = total.shape[0] // 2
    core = lax.axis_index("gy") & 1
    kept[...] = total[pl.ds(pl.multiple_of(core * rows, rows), rows), :]
    given[...] = total[pl.ds(pl.multiple_of((1 - core) * rows, rows), rows), :]


def output(pieces, upper, lower, out_scale, ffn):
    n = 2 * (len(pieces) - 1)
    rows, width = ffn.shape
    return pl.pallas_call(
        functools.partial(output_kernel, n),
        in_specs=[VMEM] * (len(pieces) + 4),
        out_specs=[VMEM] * 2,
        out_shape=[jax.ShapeDtypeStruct((rows // 2, width), f32)] * 2,
        scratch_shapes=[pltpu.VMEM((rows, width), f32), pltpu.VMEM((n,) + pieces[0].shape[1:], f32)],
        compiler_params=params(20),
        name="output",
    )(*pieces, upper, lower, out_scale.reshape(-1, LANES), ffn)


def body(n_gx, n_gy, residual, ffn_partial, norm_gain, smooth_scale, w_query, query_scale, w_keyval, keyval_scale,
         key_cache, value_cache, key_scale, value_scale, lengths, w_out, out_scale):
    gy = lax.axis_index("gy")
    rows = residual.shape[0]
    requests = rows // n_gy
    parts = project(n_gx, residual, norm_gain, smooth_scale, w_query, w_keyval)
    head = w_out.shape[0] * 11 // 16
    upper = fetch(parts[0], w_out, 0, head)
    total = trade(parts, "gx", n_gx)
    total[0], upper = lax.optimization_barrier((total[0], upper))
    pieces = spread(norm(total, query_scale, keyval_scale), n_gx)
    parts = attend(n_gx, pieces, lengths, key_cache, value_cache, key_scale, value_scale)
    lower = fetch(parts[0], w_out, head, w_out.shape[0] - head)
    total = trade([part.astype(jnp.float16) for part in parts], "gx", n_gx)
    total = [parts[0]] + [part.astype(f32) for part in total[1:]]
    total[0], lower = lax.optimization_barrier((total[0], lower))
    pieces = spread(merge(total, requests), n_gx)
    kept, given = output(pieces, upper, lower, out_scale, ffn_partial[0])
    core = gy & 1
    chip = kept + swap(given, "gy", n_gy, 1)
    other = swap((chip * (1 / SHRINK)).astype(jnp.float16), "gy", n_gy, 2)
    whole = chip + other.astype(f32) * SHRINK
    mine = lax.dynamic_slice_in_dim(residual, core * (rows // 2), rows // 2, 0)
    mine = (mine.astype(f32) + whole).astype(bf16)
    return jnp.concatenate(ordered([mine, swap(mine, "gy", n_gy, 1)], core))


def joined(value, axis, join):
    pieces = jax.tree.map(lambda part: lax.all_gather(part, axis), value)
    head = jax.tree.map(lambda part: part[0], pieces)
    tail = jax.tree.map(lambda part: part[1:], pieces)
    subtotal, _ = lax.scan(lambda subtotal, piece: (join(subtotal, piece), None), head, tail)
    return subtotal


def combine(former, latter):
    top = jnp.maximum(former[0], latter[0])
    first_factor = jnp.exp(former[0] - top)
    second_factor = jnp.exp(latter[0] - top)
    total = former[1] * first_factor + latter[1] * second_factor
    mixed = former[2] * first_factor[..., None] + latter[2] * second_factor[..., None]
    return (top, total, mixed)


def plain_body(
    residual,
    ffn_partial,
    norm_gain,
    smooth_scale,
    w_query,
    query_scale,
    w_keyval,
    keyval_scale,
    key_cache,
    value_cache,
    key_scale,
    value_scale,
    lengths,
    w_out,
    out_scale,
):
    widened = residual.astype(jnp.float32)
    ffn_total = lax.psum(ffn_partial[0], "gy")
    squares = jnp.sum(widened * widened, axis=1)
    smoothed = (widened * (norm_gain / smooth_scale)).astype(jnp.bfloat16)
    query_part = jnp.dot(smoothed, w_query, preferred_element_type=jnp.float32) * query_scale
    keyval_part = jnp.dot(smoothed, w_keyval, preferred_element_type=jnp.float32) * keyval_scale
    query_sum, keyval_sum, square_sum = lax.psum((query_part, keyval_part, squares), "gx")
    row_scale = lax.rsqrt(square_sum / D + EPSILON)[:, None]
    query_rows = (row_scale * query_sum).astype(jnp.bfloat16)
    keyval_rows = (row_scale * keyval_sum).astype(jnp.bfloat16)
    query_vectors, keyvals = (
        lax.all_to_all(query_rows, "gy", split_axis=0, concat_axis=1, tiled=True),
        lax.all_to_all(keyval_rows, "gy", split_axis=0, concat_axis=1, tiled=True),
    )
    requests = query_vectors.shape[0]
    local = key_cache.shape[2]
    group = HEADS // KV_HEADS
    score_multiplier = HEAD_DIM ** (-0.5)
    grouped = query_vectors.reshape(requests, KV_HEADS, group, HEAD_DIM)
    fresh_key_rows = keyvals[:, : KV_HEADS * HEAD_DIM].reshape(requests, KV_HEADS, HEAD_DIM)
    fresh_value_rows = keyvals[:, KV_HEADS * HEAD_DIM :].reshape(requests, KV_HEADS, HEAD_DIM)
    logit_scores = jnp.einsum(
        "rgqd,rgsd->rgqs", grouped, key_cache, preferred_element_type=jnp.float32
    )
    logit_scores = logit_scores * key_scale[:, :, None, :] * score_multiplier
    position = lax.axis_index("gx") * local + jnp.arange(local, dtype=jnp.int32)
    visible = (position[None, :] < lengths[:, None])[:, None, None, :]
    logit_scores = jnp.where(visible, logit_scores, NEGATIVE)
    local_top = jnp.max(logit_scores, axis=-1)
    weights = jnp.where(visible, jnp.exp(logit_scores - local_top[..., None]), 0.0)
    local_total = jnp.sum(weights, axis=-1)
    scaled = (weights * value_scale[:, :, None, :]).astype(jnp.bfloat16)
    local_mixed = jnp.einsum(
        "rgqs,rgsd->rgqd", scaled, value_cache, preferred_element_type=jnp.float32
    )
    top, total, mixed = joined((local_top, local_total, local_mixed), "gx", combine)
    own = (
        jnp.einsum("rgqd,rgd->rgq", grouped, fresh_key_rows, preferred_element_type=jnp.float32)
        * score_multiplier
    )
    largest = jnp.maximum(top, own)
    old_factor = jnp.exp(top - largest)
    own_weight = jnp.exp(own - largest)
    total = total * old_factor + own_weight
    mixed = (
        mixed * old_factor[..., None]
        + own_weight[..., None] * fresh_value_rows.astype(jnp.float32)[:, :, None, :]
    )
    attended = (mixed / total[..., None]).astype(jnp.bfloat16).reshape(requests, HEADS * HEAD_DIM)
    head_block = lax.all_to_all(attended, "gy", split_axis=1, concat_axis=0, tiled=True)
    projected = jnp.dot(head_block, w_out, preferred_element_type=jnp.float32) * out_scale
    attention_total = lax.psum(projected, "gy")
    new_residual = (widened + ffn_total + attention_total).astype(jnp.bfloat16)
    return new_residual


def solution(mesh):
    placed = (
        P("rep", "gx"), P("gy", "rep", "gx"), P("gx"), P("gx"), P("gx", "gy"), P("gy"), P("gx", "gy"), P("gy"),
        P(("rep", "gy"), None, "gx", None), P(("rep", "gy"), None, "gx", None),
        P(("rep", "gy"), None, "gx"), P(("rep", "gy"), None, "gx"), P(("rep", "gy")), P("gy", "gx"), P("gx"),
    )
    n_gx, n_gy = mesh.shape["gx"], mesh.shape["gy"]

    def run(*arrays):
        if n_gx == 4 and n_gy == 4:
            return body(n_gx, n_gy, *arrays)
        return plain_body(*arrays)

    return jax.shard_map(run, mesh=mesh, in_specs=placed, out_specs=P("rep", "gx"), check_vma=False)
```
